256 devices in a mesh: dp: 32 (over y_hi, z, core), tensor: 8 (over y_lo, x).
Axes of the slice: x: 4, y: 4 (y_hi: 2, y_lo: 2; y = y_hi * 2 + y_lo), z: 8, core: 2. Of those that a mesh axis runs over, the one named last changes fastest.
Arguments:
- tokens: bfloat16 [4096, 6144], P('dp', 'tensor'), may hold values from -6 to 6
- weight: bfloat16 [6144, 28672], P('tensor', 'dp'), may hold values from -0.078125 to 0.078125
- factors: float32 [4, 64, 6144], P(None, None, 'tensor'), may hold values from -0.6 to 0.6
- cotangent: bfloat16 [4096, 28672], P('tensor', 'dp'), may hold values from -6 to 6
Outputs:
- projected: bfloat16 [4096, 28672], P('tensor', 'dp')
- grad_tokens: float32 [4096, 6144], P('dp', 'tensor')
- grad_factors: float32 [4, 64, 6144], P(None, None, 'tensor')
The draws below stay inside these ranges and needn't reach their ends.
All inputs are finite; a program needn't handle non-finite values.
Results may differ from the reference program's by a relative error of at most 0.0049.
Values may be sent and summed in bfloat16 or wider, within the bound.
A program may use at most 128 MiB of HBM per device.

```python
import jax
import jax.numpy as jnp
from jax import lax

D = 6144
FF = 28672
BLOCK = 64
SECTIONS = 4
TOKENS = 4096
N_DP = 32
N_TENSOR = 8


def level_of(stream_key, dims, cuts, least, high):
    loudness = 1.0
    for position, blocks in cuts:
        draws = jax.random.uniform(jax.random.fold_in(jax.random.fold_in(stream_key, 6), position), (blocks,), jnp.float32, least / len(cuts), high / len(cuts))
        loudness = loudness * jnp.repeat(jnp.exp(draws), dims[position] // blocks).reshape((-1,) + (1,) * (len(dims) - 1 - position))
    return loudness


def scatter_about(stream_key, shape, scale, limit, cuts=(), dtype=jnp.bfloat16):
    values = scale * jax.random.normal(stream_key, shape, jnp.float32)
    if cuts:
        values = values * level_of(stream_key, shape, cuts, -0.22, 0.18)
    return jnp.clip(values, -limit, limit).astype(dtype)


def setup_inputs(seed: int = 0) -> dict:
    arg_keys = jax.random.split(jax.random.key(seed), 5)
    tokens = scatter_about(arg_keys[0], (TOKENS, D), 1.0, 6.0, ((0, 32), (1, 8)))
    weight = scatter_about(arg_keys[1], (D, FF), D ** -0.5, 0.078125, ((0, 8), (1, 32)))
    factors = scatter_about(arg_keys[2], (SECTIONS, BLOCK, D), 0.1, 0.6, ((2, 8),), jnp.float32)
    cotangent = scatter_about(arg_keys[3], (TOKENS, FF), 1.0, 6.0, ((0, 8), (1, 32)))
    return {"tokens": tokens, "weight": weight, "factors": factors, "cotangent": cotangent}


def apply_factor(field, coeffs, section):
    rows, width = field.shape
    half = BLOCK // 2
    groups = N_TENSOR
    span = width // groups
    hi = lax.Precision.HIGHEST
    if section == 0:
        count = width // BLOCK
        inputs = field.reshape(rows, count, BLOCK)
        added = jnp.einsum('tqk,kqc->tqc', inputs, coeffs.reshape(BLOCK, count, BLOCK), precision=hi)
    elif section == 1:
        count = width // (2 * BLOCK)
        viewed = field.reshape(rows, count, 2, 2, half)
        inputs = viewed.transpose(0, 1, 3, 2, 4).reshape(rows, count, 2, BLOCK)
        added = jnp.einsum('tqak,kqbaw->tqbaw', inputs, coeffs.reshape(BLOCK, count, 2, 2, half), precision=hi)
    elif section == 2:
        viewed = field.reshape(rows, groups // 2, 2, span // half, half)
        inputs = viewed.transpose(0, 1, 3, 2, 4).reshape(rows, groups // 2, span // half, BLOCK)
        added = jnp.einsum('tghk,kgbhw->tgbhw', inputs, coeffs.reshape(BLOCK, groups // 2, 2, span // half, half), precision=hi)
    else:
        viewed = field.reshape(rows, 2, groups // 2, span // half, half)
        inputs = viewed.transpose(0, 2, 3, 1, 4).reshape(rows, groups // 2, span // half, BLOCK)
        added = jnp.einsum('trhk,kbrhw->tbrhw', inputs, coeffs.reshape(BLOCK, 2, groups // 2, span // half, half), precision=hi)
    return field + added.reshape(rows, width)

def butterfly(field, factors):
    for section in range(SECTIONS):
        field = apply_factor(field, factors[section], section)
    return field

def reference(tokens, weight, factors, cotangent):
    start = tokens.astype(jnp.float32)
    turned, pull = jax.vjp(butterfly, start, factors)
    rotated = turned.astype(jnp.bfloat16)
    span = D // N_TENSOR
    total = jnp.zeros((TOKENS, FF), jnp.float32)
    for group in range(N_TENSOR):
        part = jnp.dot(rotated[:, group * span:(group + 1) * span].astype(jnp.float32), weight[group * span:(group + 1) * span].astype(jnp.float32), preferred_element_type=jnp.float32)
        total = total + part
    projected = total.astype(jnp.bfloat16)
    slice_width = FF // N_DP
    back = jnp.zeros((TOKENS, D), jnp.float32)
    for owner in range(N_DP):
        lo_col = owner * slice_width
        piece = jnp.dot(cotangent[:, lo_col:lo_col + slice_width].astype(jnp.float32), weight[:, lo_col:lo_col + slice_width].astype(jnp.float32).T, preferred_element_type=jnp.float32)
        back = back + piece
    grad_tokens, grad_factors = pull(back)
    return (projected, grad_tokens, grad_factors)
```

```python
import jax
import jax.numpy as jnp
from jax import lax
from jax.experimental import pallas as pl
from jax.experimental.pallas import tpu as pltpu
from jax.sharding import PartitionSpec as P

HIGH = lax.Precision.HIGHEST
F32 = jnp.float32
BF16 = jnp.bfloat16
MESH = pl.DeviceIdType.MESH


def swapped(shard, axis, bit):
    return lax.ppermute(shard, axis, [(i, i ^ 1 << bit) for i in range(lax.axis_size(axis))])


def first_backward(grad_out, inputs, coeffs, block):
    rows, width = grad_out.shape
    count = width // block
    viewed = grad_out.reshape(rows, count, block)
    grad_coeffs = jnp.einsum("tqk,tqc->kqc", inputs, viewed, precision=HIGH).reshape(block, width)
    grad_inputs = jnp.einsum(
        "tqc,kqc->tqk", viewed, coeffs.reshape(block, count, block), precision=HIGH
    )
    return (grad_out + grad_inputs.reshape(rows, width), grad_coeffs)


def second_backward(grad_out, inputs, coeffs, block):
    rows, width = grad_out.shape
    half = block // 2
    count = width // (2 * block)
    viewed = grad_out.reshape(rows, count, 2, 2, half)
    grad_coeffs = jnp.einsum("tqak,tqbaw->kqbaw", inputs, viewed, precision=HIGH).reshape(
        block, width
    )
    grad_inputs = jnp.einsum(
        "tqbaw,kqbaw->tqak", viewed, coeffs.reshape(block, count, 2, 2, half), precision=HIGH
    )
    grad_inputs = grad_inputs.reshape(rows, count, 2, 2, half).transpose(0, 1, 3, 2, 4)
    return (grad_out + grad_inputs.reshape(rows, width), grad_coeffs)


def lower_side(bit):
    return lax.axis_index("tensor") // (1 << bit) % 2 == 0


def cross_inputs(own, partner, block, bit):
    rows, width = own.shape
    half = block // 2
    mine = own.reshape(rows, width // half, half)
    theirs = partner.reshape(rows, width // half, half)
    return jnp.where(
        lower_side(bit), jnp.concatenate([mine, theirs], 2), jnp.concatenate([theirs, mine], 2)
    )


def cross_backward(grad_out, inputs, coeffs, block, bit):
    rows, width = grad_out.shape
    half = block // 2
    viewed = grad_out.reshape(rows, width // half, half)
    grad_coeffs = jnp.einsum("thk,thw->khw", inputs, viewed, precision=HIGH).reshape(block, width)
    grad_inputs = jnp.einsum(
        "thw,khw->thk", viewed, coeffs.reshape(block, width // half, half), precision=HIGH
    )
    lower = lower_side(bit)
    own_part = jnp.where(lower, grad_inputs[:, :, :half], grad_inputs[:, :, half:])
    other_part = jnp.where(lower, grad_inputs[:, :, half:], grad_inputs[:, :, :half])
    arrived = swapped(other_part.reshape(rows, width), "tensor", bit)
    return (grad_out + own_part.reshape(rows, width) + arrived, grad_coeffs)


def hdot(a, b):
    return jnp.dot(a, b, precision=HIGH, preferred_element_type=F32)


def quarter_masks():
    r = lax.broadcasted_iota(jnp.int32, (128, 128), 0) // 32
    c = lax.broadcasted_iota(jnp.int32, (128, 128), 1) // 32
    return (r // 2 == c // 2, r % 2 == c % 2, r == c)


def local_matrix(coeffs, masks, section):
    if section == 0:
        stacked = jnp.concatenate([coeffs, coeffs], 0)
    else:
        stacked = jnp.concatenate([coeffs[:32], coeffs[:32], coeffs[32:], coeffs[32:]], 0)
    return jnp.where(masks[section], stacked, 0.0)


def cross_matrices(coeffs, masks, lower):
    first, second = coeffs[:32], coeffs[32:]
    own = jnp.where(lower, first, second)
    other = jnp.where(lower, second, first)
    return [jnp.where(masks[2], jnp.concatenate([part] * 4, 0), 0.0) for part in (own, other)]


def local_section(src, dst, factors, masks, section):
    for q in range(6):
        cols = pl.ds(128 * q, 128)
        field = src[:, cols].astype(F32)
        dst[:, cols] = field + hdot(field, local_matrix(factors[section, :, cols], masks, section))


def cross_section(src, partner, put, factors, masks, section, lower):
    for q in range(6):
        cols = pl.ds(128 * q, 128)
        own, other = cross_matrices(factors[section, :, cols], masks, lower)
        field = src[:, cols]
        put(cols, field + hdot(field, own) + hdot(partner[:, cols].astype(F32), other))


def main_kernel(
    tokens, w_own, factors, w_hbm, cot_hbm,
    proj, z1, z2, p2, z3, p3, g4,
    zsend, rot, R, cotG, w_oth, bsib, bsib_in, bown, up_out, up_in, dn_out, dn_in,
    pbuf, px_out, px_in, gsend, gin,
    loc_sem, sx, rx, sy, ry, sc, rc, sw, rw, sys, yr, sR, rR, sS, rS, sB, rB, sZ, rZ, sP, rP,
    sG, rG,
):
    dp, tn = lax.axis_index("dp"), lax.axis_index("tensor")
    core, z, yh = dp % 2, dp // 2 % 8, dp // 16
    x, yl = tn % 4, tn // 4

    def dev(yh=yh, z=z, core=core, yl=yl, x=x):
        return (yh * 16 + z * 2 + core, yl * 4 + x)

    right, left = dev(x=(x + 1) % 4), dev(x=(x + 3) % 4)
    xpair = dev(x=x + 1 - 2 * (x % 2))
    ypair = dev(yl=1 - yl)
    sibling = dev(core=1 - core)
    above, below = dev(z=(z + 1) % 8), dev(z=(z + 7) % 8)
    diagonal = yh == yl

    sent = []

    def rcopy(src, dst, ssem, rsem, to):
        return pltpu.make_async_remote_copy(
            src_ref=src, dst_ref=dst, send_sem=ssem, recv_sem=rsem,
            device_id=to, device_id_type=MESH,
        )

    def send(src, dst, ssem, rsem, to):
        copy = rcopy(src, dst, ssem, rsem, to)
        copy.start()
        sent.append(copy)

    def arrived(dst, rsem):
        rcopy(dst, dst, rsem, rsem, sibling).wait_recv()

    barrier = pltpu.get_barrier_semaphore()
    for peer in (right, left, ypair, sibling, above, below):
        pl.semaphore_signal(barrier, inc=1, device_id=peer, device_id_type=MESH)
    for peer, here in (
        (dev(yh=0, yl=yh), (yh == 0) & diagonal),
        (dev(yh=1, yl=yh), (yh == 1) & diagonal),
        (dev(yh=yl, yl=0), (yl == 0) & diagonal),
        (dev(yh=yl, yl=1), (yl == 1) & diagonal),
    ):
        @pl.when(jnp.logical_not(here))
        def _():
            pl.semaphore_signal(barrier, inc=1, device_id=peer, device_id_type=MESH)
    pl.semaphore_wait(barrier, 10 - 2 * diagonal.astype(jnp.int32))

    def half(index):
        return cotG.at[index]

    own_cot = [pltpu.make_async_copy(cot_hbm.at[pl.ds(256 * i, 256)], half(2 * x + i), loc_sem.at[i]) for i in range(2)]
    for copy in own_cot:
        copy.start()

    masks = quarter_masks()
    local_section(tokens, z1, factors, masks, 0)
    local_section(z1, z2, factors, masks, 1)
    zsend[0] = z2[...].astype(BF16)
    send(zsend.at[0], zsend.at[2], sx.at[0], rx.at[0], xpair)

    for i, to in ((0, right), (1, left), (1, right), (0, left)):
        n = i + (0 if to is right else 2)
        send(cot_hbm.at[pl.ds(256 * i, 256)], half(2 * x + i), sc.at[n], rc.at[n], to)

    def send_w(i):
        rows = pl.ds(256 * i, 256)
        send(w_hbm.at[rows], w_oth.at[rows], sw.at[i], rw.at[i], ypair)

    send_w(0)
    arrived(zsend.at[2], rx.at[0])
    p2[...] = zsend[2].astype(F32)

    def put3(cols, value):
        z3[:, cols] = value
        zsend[1, :, cols] = value.astype(BF16)

    cross_section(z2, p2, put3, factors, masks, 2, x % 2 == 0)
    send(zsend.at[1], zsend.at[3], sy.at[0], ry.at[0], ypair)
    arrived(zsend.at[3], ry.at[0])
    p3[...] = zsend[3].astype(F32)

    def put4(cols, value):
        rot[:, cols] = value.astype(BF16)

    cross_section(z3, p3, put4, factors, masks, 3, yl == 0)

    slot = (yl + yh) % 2
    for b in range(2):
        copy = rcopy(rot, R.at[z, slot, core], sys.at[b], yr.at[slot], dev(yh=b, yl=yh))
        pl.when(jnp.logical_not((yh == b) & diagonal))(copy.start)

    @pl.when(diagonal)
    def _():
        R[z, 0, core] = rot[...]

    send_w(1)
    send_w(2)

    def spread(zz, s, up, down, k):
        block = R.at[zz, s, core]
        if up:
            send(block, block, sR.at[0, k, s], rR.at[0, k, s], above)
        if down:
            send(block, block, sR.at[1, k, s], rR.at[1, k, s], below)
        send(block, block, sS.at[zz, s], rS.at[zz, s], sibling)

    @pl.when(jnp.logical_not(diagonal))
    def _():
        arrived(R.at[z, 0, core], yr.at[0])
    spread(z, 0, True, True, 0)
    arrived(R.at[z, 1, core], yr.at[1])
    spread(z, 1, True, True, 0)

    def step(k):
        lo, hi = (z + 8 - k) % 8, (z + k) % 8
        for s in range(2):
            arrived(R.at[lo, s, core], rR.at[0, k - 1, s])
            spread(lo, s, k < 3 or s == 0, False, k)
            arrived(R.at[hi, s, core], rR.at[1, k - 1, s])
            spread(hi, s, False, k < 3 or s == 1, k)

    step(1)
    xl, xr = (x + 3) % 4, (x + 1) % 4
    arrived(half(2 * xl), rc.at[0])
    send(half(2 * xl), half(2 * xl), sc.at[4], rc.at[4], right)
    arrived(half(2 * xr + 1), rc.at[3])
    send(half(2 * xr + 1), half(2 * xr + 1), sc.at[5], rc.at[5], left)
    step(2)
    step(3)

    xo = (x + 2) % 4
    arrived(half(2 * xl + 1), rc.at[1])
    arrived(half(2 * xr), rc.at[2])
    arrived(half(2 * xo), rc.at[4])
    arrived(half(2 * xo + 1), rc.at[5])
    for copy in own_cot:
        copy.wait()
    for i in range(3):
        arrived(w_oth.at[pl.ds(256 * i, 256)], rw.at[i])

    def back_block(n, carry):
        zz = (z + 4 + n) % 8
        left_side = cotG[zz]
        for s, w in ((0, w_own), (1, w_oth)):
            part = lax.dot_general(left_side, w[...], (((1,), (1,)), ((), ())), preferred_element_type=F32)

            @pl.when(core == 0)
            def _():
                bown[zz, s] = part[:128]
                bsib[zz, s] = part[128:].astype(BF16)

            @pl.when(core == 1)
            def _():
                bown[zz, s] = part[128:]
                bsib[zz, s] = part[:128].astype(BF16)
        rcopy(bsib.at[zz], bsib_in.at[zz], sB.at[zz], rB.at[zz], sibling).start()
        return carry

    lax.fori_loop(0, 8, back_block, 0)

    zf = (z + 4) % 8
    arrived(R.at[zf, 0, core], rR.at[0, 3, 0])
    spread(zf, 0, False, False, 4)
    arrived(R.at[zf, 1, core], rR.at[1, 3, 1])
    spread(zf, 1, False, False, 4)

    def own_back(zz, s):
        return bown[zz, s] + bsib_in[zz, s].astype(F32)

    def back_ready(zz):
        arrived(bsib_in.at[zz], rB.at[zz])

    def ring_send(direction, n, zz, s, incoming):
        out, into = (up_out, up_in) if direction == 0 else (dn_out, dn_in)
        value = own_back(zz, s)
        if incoming is not None:
            arrived(into.at[incoming], rZ.at[direction, incoming])
            value = value + into[incoming].astype(F32)
        out[n] = value.astype(BF16)
        send(out.at[n], into.at[n], sZ.at[direction, n], rZ.at[direction, n], above if direction == 0 else below)

    def z_at(k):
        return (z + 8 + k) % 8

    back_ready(z_at(4))
    ring_send(0, 0, z_at(4), 0, None)
    ring_send(1, 0, z_at(4), 1, None)
    back_ready(z_at(3))
    back_ready(z_at(-3))
    ring_send(0, 1, z_at(3), 1, None)
    ring_send(1, 1, z_at(-3), 0, None)

    for n in range(8):
        for s in range(2):
            block = R.at[n, s, 1 - core]
            arrived(block, rS.at[n, s])

    def product(zz):
        return jnp.dot(R[zz, 0].reshape(256, 768), w_own[...], preferred_element_type=F32) + jnp.dot(
            R[zz, 1].reshape(256, 768), w_oth[...], preferred_element_type=F32
        )

    def px_send(direction, n, zz, incoming):
        value = product(zz)
        if incoming is not None:
            arrived(px_in.at[direction, incoming], rP.at[direction, incoming])
            value = value + px_in[direction, incoming].astype(F32)
        px_out[direction, n] = value.astype(BF16)
        send(px_out.at[direction, n], px_in.at[direction, n], sP.at[direction, n], rP.at[direction, n], right if direction == 0 else left)

    px_send(0, 0, 2 * xo, None)
    px_send(1, 0, 2 * xo + 1, None)
    ring_send(0, 2, z_at(3), 0, 0)
    ring_send(1, 2, z_at(-3), 1, 0)
    px_send(0, 1, 2 * xr + 1, None)
    px_send(1, 1, 2 * xl, None)
    back_ready(z_at(2))
    back_ready(z_at(-2))
    ring_send(0, 3, z_at(2), 1, 1)
    ring_send(1, 3, z_at(-2), 0, 1)
    ring_send(0, 4, z_at(2), 0, 2)
    ring_send(1, 4, z_at(-2), 1, 2)
    px_send(0, 2, 2 * xr, 0)
    px_send(1, 2, 2 * xl + 1, 0)
    back_ready(z_at(1))
    back_ready(z_at(-1))
    ring_send(0, 5, z_at(1), 1, 3)
    ring_send(1, 5, z_at(-1), 0, 3)
    ring_send(0, 6, z_at(1), 0, 4)
    ring_send(1, 6, z_at(-1), 1, 4)
    back_ready(z)
    pbuf[0] = product(2 * x)
    pbuf[1] = product(2 * x + 1)

    for s, nu, nd in ((1, 5, 6), (0, 6, 5)):
        arrived(up_in.at[nu], rZ.at[0, nu])
        arrived(dn_in.at[nd], rZ.at[1, nd])
        gsend[s] = (own_back(z, s) + up_in[nu].astype(F32) + dn_in[nd].astype(F32)).astype(BF16)
        copy = rcopy(gsend.at[s], gin.at[yh], sG.at[s], rG.at[yh], dev(yh=yl, yl=(yl + s) % 2))
        if s == 1:
            copy.start()
        else:
            pl.when(jnp.logical_not(diagonal))(copy.start)

    @pl.when(diagonal)
    def _():
        gin[yh] = gsend[0]

    for a in range(2):
        @pl.when(jnp.logical_not((yh == a) & diagonal))
        def _():
            arrived(gin.at[a], rG.at[a])
    g4[...] = gin[0].astype(F32) + gin[1].astype(F32)

    arrived(px_in.at[0, 2], rP.at[0, 2])
    arrived(px_in.at[1, 1], rP.at[1, 1])
    proj[pl.ds(0, 256), :] = (pbuf[0] + px_in[0, 2].astype(F32) + px_in[1, 1].astype(F32)).astype(BF16)
    arrived(px_in.at[0, 1], rP.at[0, 1])
    arrived(px_in.at[1, 2], rP.at[1, 2])
    proj[pl.ds(256, 256), :] = (pbuf[1] + px_in[0, 1].astype(F32) + px_in[1, 2].astype(F32)).astype(BF16)

    for copy in sent:
        copy.wait_send()
    for b in range(2):
        copy = rcopy(rot, R.at[z, slot, core], sys.at[b], yr.at[slot], dev(yh=b, yl=yh))
        pl.when(jnp.logical_not((yh == b) & diagonal))(copy.wait_send)
    for n in range(8):
        rcopy(bsib.at[n], bsib_in.at[n], sB.at[n], rB.at[n], sibling).wait_send()
    rcopy(gsend.at[1], gin.at[0], sG.at[1], rG.at[0], ypair).wait_send()
    pl.when(jnp.logical_not(diagonal))(rcopy(gsend.at[0], gin.at[0], sG.at[0], rG.at[0], ypair).wait_send)


def main_call(tokens, weight, factors, cotangent):
    V = pltpu.VMEM
    D = pltpu.SemaphoreType.DMA
    field = jax.ShapeDtypeStruct((128, 768), F32)
    vm = pl.BlockSpec(memory_space=pltpu.VMEM)
    hbm = pl.BlockSpec(memory_space=pl.ANY)
    return pl.pallas_call(
        main_kernel,
        out_shape=(jax.ShapeDtypeStruct((512, 896), BF16),) + (field,) * 6,
        in_specs=[vm, vm, vm, hbm, hbm],
        out_specs=(vm,) * 7,
        scratch_shapes=[
            V((4, 128, 768), BF16),
            V((128, 768), BF16),
            V((8, 2, 2, 128, 768), BF16),
            V((8, 256, 896), BF16),
            V((768, 896), BF16),
            V((8, 2, 128, 768), BF16),
            V((8, 2, 128, 768), BF16),
            V((8, 2, 128, 768), F32),
            V((7, 128, 768), BF16),
            V((7, 128, 768), BF16),
            V((7, 128, 768), BF16),
            V((7, 128, 768), BF16),
            V((2, 256, 896), F32),
            V((2, 3, 256, 896), BF16),
            V((2, 3, 256, 896), BF16),
            V((2, 128, 768), BF16),
            V((2, 128, 768), BF16),
            D((2,)),
            D((1,)), D((1,)), D((1,)), D((1,)),
            D((6,)), D((6,)), D((3,)), D((3,)),
            D((2,)), D((2,)),
            D((2, 4, 2)), D((2, 4, 2)),
            D((8, 2)), D((8, 2)),
            D((8,)), D((8,)),
            D((2, 7)), D((2, 7)),
            D((2, 3)), D((2, 3)),
            D((2,)), D((2,)),
        ],
        compiler_params=pltpu.CompilerParams(
            collective_id=0, has_side_effects=True, vmem_limit_bytes=56 * 1024 * 1024
        ),
        name="rotate_project",
    )(tokens, weight, factors, weight, cotangent)


def per_device(tokens, weight, factors, cotangent):
    block = factors.shape[1]
    top_bit = lax.axis_size("tensor").bit_length() - 2
    projected, z1, z2, p2, z3, p3, back = main_call(tokens, weight, factors, cotangent)
    rows, width = tokens.shape
    inputs0 = tokens.astype(F32).reshape(rows, width // block, block)
    inputs1 = z1.reshape(rows, width // (2 * block), 2, 2, block // 2).transpose(0, 1, 3, 2, 4)
    inputs1 = inputs1.reshape(rows, width // (2 * block), 2, block)
    inputs2 = cross_inputs(z2, p2, block, 0)
    inputs3 = cross_inputs(z3, p3, block, top_bit)
    grad_now, grad_three = cross_backward(back, inputs3, factors[3], block, top_bit)
    grad_now, grad_two = cross_backward(grad_now, inputs2, factors[2], block, 0)
    grad_now, grad_one = second_backward(grad_now, inputs1, factors[1], block)
    grad_now, grad_zero = first_backward(grad_now, inputs0, factors[0], block)
    stacked = jnp.stack([grad_zero, grad_one, grad_two, grad_three])
    stacked = lax.psum(stacked, "dp")
    return (projected, grad_now, stacked)


def solution(mesh):
    placed = (P("dp", "tensor"), P("tensor", "dp"), P(None, None, "tensor"), P("tensor", "dp"))
    return jax.shard_map(
        per_device,
        mesh=mesh,
        in_specs=placed,
        out_specs=(P("tensor", "dp"), P("dp", "tensor"), P(None, None, "tensor")),
        check_vma=False,
    )
```

```python
import jax
import jax.numpy as jnp
from jax import lax
from jax.experimental import pallas as pl
from jax.experimental.pallas import tpu as pltpu
from jax.sharding import PartitionSpec as P

HIGH = lax.Precision.HIGHEST
F32 = jnp.float32
BF16 = jnp.bfloat16
MESH = pl.DeviceIdType.MESH


def hdot(a, b):
    return jnp.dot(a, b, precision=HIGH, preferred_element_type=F32)


def hdot_nt(a, b):
    return lax.dot_general(a, b, (((1,), (1,)), ((), ())), precision=HIGH, preferred_element_type=F32)


def hdot_tn(a, b):
    return lax.dot_general(a, b, (((0,), (0,)), ((), ())), precision=HIGH, preferred_element_type=F32)


def quarter_masks():
    r = lax.broadcasted_iota(jnp.int32, (128, 128), 0) // 32
    c = lax.broadcasted_iota(jnp.int32, (128, 128), 1) // 32
    return (r // 2 == c // 2, r % 2 == c % 2, r == c)


def local_matrix(coeffs, masks, section):
    if section == 0:
        stacked = jnp.concatenate([coeffs, coeffs], 0)
    else:
        stacked = jnp.concatenate([coeffs[:32], coeffs[:32], coeffs[32:], coeffs[32:]], 0)
    return jnp.where(masks[section], stacked, 0.0)


def cross_matrices(coeffs, masks, lower):
    first, second = coeffs[:32], coeffs[32:]
    own = jnp.where(lower, first, second)
    other = jnp.where(lower, second, first)
    return [jnp.where(masks[2], jnp.concatenate([part] * 4, 0), 0.0) for part in (own, other)]


def local_section(src, dst, factors, masks, section):
    for q in range(6):
        cols = pl.ds(128 * q, 128)
        field = src[:, cols].astype(F32)
        dst[:, cols] = field + hdot(field, local_matrix(factors[section, :, cols], masks, section))


def cross_section(src, partner, put, factors, masks, section, lower):
    for q in range(6):
        cols = pl.ds(128 * q, 128)
        own, other = cross_matrices(factors[section, :, cols], masks, lower)
        field = src[:, cols]
        put(cols, field + hdot(field, own) + hdot(partner[:, cols].astype(F32), other))


def fold_cross(full, masks):
    full = jnp.where(masks[2], full, 0.0)
    return full[:32] + full[32:64] + full[64:96] + full[96:]


def main_kernel(
    tokens, w_own, factors, w_hbm, cot_hbm,
    proj, grad_tokens, grad_factors,
    z1, z2, p2, z3, p3, ga, gb, gf, cin, gh, ain, res, fout,
    zsend, rot, R, cotG, w_oth, bsib, bsib_in, bown, up_out, up_in, dn_out, dn_in,
    pbuf, px_out, px_in, gsend, gin,
    loc_sem, sx, rx, sy, ry, sc, rc, sw, rw, sys, yr, sR, rR, sS, rS, sB, rB, sZ, rZ, sP, rP,
    sG, rG, sC, rC, sA, rA, sF, rF, sH, rH,
):
    dp, tn = lax.axis_index("dp"), lax.axis_index("tensor")
    core, z, yh = dp % 2, dp // 2 % 8, dp // 16
    x, yl = tn % 4, tn // 4

    def dev(yh=yh, z=z, core=core, yl=yl, x=x):
        return (yh * 16 + z * 2 + core, yl * 4 + x)

    right, left = dev(x=(x + 1) % 4), dev(x=(x + 3) % 4)
    xpair = dev(x=x + 1 - 2 * (x % 2))
    ypair = dev(yl=1 - yl)
    sibling = dev(core=1 - core)
    above, below = dev(z=(z + 1) % 8), dev(z=(z + 7) % 8)
    diagonal = yh == yl

    sent = []

    def rcopy(src, dst, ssem, rsem, to):
        return pltpu.make_async_remote_copy(
            src_ref=src, dst_ref=dst, send_sem=ssem, recv_sem=rsem,
            device_id=to, device_id_type=MESH,
        )

    def send(src, dst, ssem, rsem, to):
        copy = rcopy(src, dst, ssem, rsem, to)
        copy.start()
        sent.append(copy)

    def arrived(dst, rsem):
        rcopy(dst, dst, rsem, rsem, sibling).wait_recv()

    barrier = pltpu.get_barrier_semaphore()
    for peer in (right, left, ypair, sibling):
        pl.semaphore_signal(barrier, inc=1, device_id=peer, device_id_type=MESH)
    chip = yh * 8 + z

    def chip_dev(index):
        return dev(yh=index // 8, z=index % 8)

    def greet(r, carry):
        pl.semaphore_signal(barrier, inc=1, device_id=chip_dev((chip + r) % 16), device_id_type=MESH)
        return carry

    lax.fori_loop(1, 16, greet, 0)
    for peer, here in (
        (dev(yh=0, yl=yh), (yh == 0) & diagonal),
        (dev(yh=1, yl=yh), (yh == 1) & diagonal),
        (dev(yh=yl, yl=0), (yl == 0) & diagonal),
        (dev(yh=yl, yl=1), (yl == 1) & diagonal),
    ):
        @pl.when(jnp.logical_not(here))
        def _():
            pl.semaphore_signal(barrier, inc=1, device_id=peer, device_id_type=MESH)
    pl.semaphore_wait(barrier, 23 - 2 * diagonal.astype(jnp.int32))

    def half(index):
        return cotG.at[index]

    own_cot = [pltpu.make_async_copy(cot_hbm.at[pl.ds(256 * i, 256)], half(2 * x + i), loc_sem.at[i]) for i in range(2)]
    for copy in own_cot:
        copy.start()

    masks = quarter_masks()
    local_section(tokens, z1, factors, masks, 0)
    local_section(z1, z2, factors, masks, 1)
    zsend[0] = z2[...].astype(BF16)
    send(zsend.at[0], zsend.at[2], sx.at[0], rx.at[0], xpair)

    for i, to in ((0, right), (1, left), (1, right), (0, left)):
        n = i + (0 if to is right else 2)
        send(cot_hbm.at[pl.ds(256 * i, 256)], half(2 * x + i), sc.at[n], rc.at[n], to)

    def send_w(i):
        rows = pl.ds(256 * i, 256)
        send(w_hbm.at[rows], w_oth.at[rows], sw.at[i], rw.at[i], ypair)

    send_w(0)
    arrived(zsend.at[2], rx.at[0])
    p2[...] = zsend[2].astype(F32)

    def put3(cols, value):
        z3[:, cols] = value
        zsend[1, :, cols] = value.astype(BF16)

    cross_section(z2, p2, put3, factors, masks, 2, x % 2 == 0)
    send(zsend.at[1], zsend.at[3], sy.at[0], ry.at[0], ypair)
    arrived(zsend.at[3], ry.at[0])
    p3[...] = zsend[3].astype(F32)

    def put4(cols, value):
        rot[:, cols] = value.astype(BF16)

    cross_section(z3, p3, put4, factors, masks, 3, yl == 0)

    slot = (yl + yh) % 2
    for b in range(2):
        copy = rcopy(rot, R.at[z, slot, core], sys.at[b], yr.at[slot], dev(yh=b, yl=yh))
        pl.when(jnp.logical_not((yh == b) & diagonal))(copy.start)

    @pl.when(diagonal)
    def _():
        R[z, 0, core] = rot[...]

    send_w(1)
    send_w(2)

    def spread(zz, s, up, down, k):
        block = R.at[zz, s, core]
        if up:
            send(block, block, sR.at[0, k, s], rR.at[0, k, s], above)
        if down:
            send(block, block, sR.at[1, k, s], rR.at[1, k, s], below)
        send(block, block, sS.at[zz, s], rS.at[zz, s], sibling)

    @pl.when(jnp.logical_not(diagonal))
    def _():
        arrived(R.at[z, 0, core], yr.at[0])
    spread(z, 0, True, True, 0)
    arrived(R.at[z, 1, core], yr.at[1])
    spread(z, 1, True, True, 0)

    def step(k):
        lo, hi = (z + 8 - k) % 8, (z + k) % 8
        for s in range(2):
            arrived(R.at[lo, s, core], rR.at[0, k - 1, s])
            spread(lo, s, k < 3 or s == 0, False, k)
            arrived(R.at[hi, s, core], rR.at[1, k - 1, s])
            spread(hi, s, False, k < 3 or s == 1, k)

    step(1)
    xl, xr = (x + 3) % 4, (x + 1) % 4
    arrived(half(2 * xl), rc.at[0])
    send(half(2 * xl), half(2 * xl), sc.at[4], rc.at[4], right)
    arrived(half(2 * xr + 1), rc.at[3])
    send(half(2 * xr + 1), half(2 * xr + 1), sc.at[5], rc.at[5], left)
    step(2)
    step(3)

    xo = (x + 2) % 4
    arrived(half(2 * xl + 1), rc.at[1])
    arrived(half(2 * xr), rc.at[2])
    arrived(half(2 * xo), rc.at[4])
    arrived(half(2 * xo + 1), rc.at[5])
    for copy in own_cot:
        copy.wait()
    for i in range(3):
        arrived(w_oth.at[pl.ds(256 * i, 256)], rw.at[i])

    def back_block(n, carry):
        zz = (z + 4 + n) % 8
        left_side = cotG[zz]
        for s, w in ((0, w_own), (1, w_oth)):
            part = lax.dot_general(left_side, w[...], (((1,), (1,)), ((), ())), preferred_element_type=F32)

            @pl.when(core == 0)
            def _():
                bown[zz, s] = part[:128]
                bsib[zz, s] = part[128:].astype(BF16)

            @pl.when(core == 1)
            def _():
                bown[zz, s] = part[128:]
                bsib[zz, s] = part[:128].astype(BF16)
        rcopy(bsib.at[zz], bsib_in.at[zz], sB.at[zz], rB.at[zz], sibling).start()
        return carry

    lax.fori_loop(0, 8, back_block, 0)

    zf = (z + 4) % 8
    arrived(R.at[zf, 0, core], rR.at[0, 3, 0])
    spread(zf, 0, False, False, 4)
    arrived(R.at[zf, 1, core], rR.at[1, 3, 1])
    spread(zf, 1, False, False, 4)

    def own_back(zz, s):
        return bown[zz, s] + bsib_in[zz, s].astype(F32)

    def back_ready(zz):
        arrived(bsib_in.at[zz], rB.at[zz])

    def ring_send(direction, n, zz, s, incoming):
        out, into = (up_out, up_in) if direction == 0 else (dn_out, dn_in)
        value = own_back(zz, s)
        if incoming is not None:
            arrived(into.at[incoming], rZ.at[direction, incoming])
            value = value + into[incoming].astype(F32)
        out[n] = value.astype(BF16)
        send(out.at[n], into.at[n], sZ.at[direction, n], rZ.at[direction, n], above if direction == 0 else below)

    def z_at(k):
        return (z + 8 + k) % 8

    back_ready(z_at(4))
    ring_send(0, 0, z_at(4), 0, None)
    ring_send(1, 0, z_at(4), 1, None)
    back_ready(z_at(3))
    back_ready(z_at(-3))
    ring_send(0, 1, z_at(3), 1, None)
    ring_send(1, 1, z_at(-3), 0, None)

    for n in range(8):
        for s in range(2):
            block = R.at[n, s, 1 - core]
            arrived(block, rS.at[n, s])

    def product(zz):
        return jnp.dot(R[zz, 0].reshape(256, 768), w_own[...], preferred_element_type=F32) + jnp.dot(
            R[zz, 1].reshape(256, 768), w_oth[...], preferred_element_type=F32
        )

    def px_send(direction, n, zz, incoming):
        value = product(zz)
        if incoming is not None:
            arrived(px_in.at[direction, incoming], rP.at[direction, incoming])
            value = value + px_in[direction, incoming].astype(F32)
        px_out[direction, n] = value.astype(BF16)
        send(px_out.at[direction, n], px_in.at[direction, n], sP.at[direction, n], rP.at[direction, n], right if direction == 0 else left)

    px_send(0, 0, 2 * xo, None)
    px_send(1, 0, 2 * xo + 1, None)
    ring_send(0, 2, z_at(3), 0, 0)
    ring_send(1, 2, z_at(-3), 1, 0)
    px_send(0, 1, 2 * xr + 1, None)
    px_send(1, 1, 2 * xl, None)
    back_ready(z_at(2))
    back_ready(z_at(-2))
    ring_send(0, 3, z_at(2), 1, 1)
    ring_send(1, 3, z_at(-2), 0, 1)
    ring_send(0, 4, z_at(2), 0, 2)
    ring_send(1, 4, z_at(-2), 1, 2)
    px_send(0, 2, 2 * xr, 0)
    px_send(1, 2, 2 * xl + 1, 0)
    back_ready(z_at(1))
    back_ready(z_at(-1))
    ring_send(0, 5, z_at(1), 1, 3)
    ring_send(1, 5, z_at(-1), 0, 3)
    ring_send(0, 6, z_at(1), 0, 4)
    ring_send(1, 6, z_at(-1), 1, 4)
    back_ready(z)
    pbuf[0] = product(2 * x)
    pbuf[1] = product(2 * x + 1)

    for s, nu, nd in ((1, 5, 6), (0, 6, 5)):
        arrived(up_in.at[nu], rZ.at[0, nu])
        arrived(dn_in.at[nd], rZ.at[1, nd])
        gsend[s] = (own_back(z, s) + up_in[nu].astype(F32) + dn_in[nd].astype(F32)).astype(BF16)
        copy = rcopy(gsend.at[s], gin.at[yh], sG.at[s], rG.at[yh], dev(yh=yl, yl=(yl + s) % 2))
        if s == 1:
            copy.start()
        else:
            pl.when(jnp.logical_not(diagonal))(copy.start)

    @pl.when(diagonal)
    def _():
        gin[yh] = gsend[0]

    for a in range(2):
        @pl.when(jnp.logical_not((yh == a) & diagonal))
        def _():
            arrived(gin.at[a], rG.at[a])
    ga[...] = gin[0].astype(F32) + gin[1].astype(F32)

    def reduce_start(s):
        send(gf.at[s, pl.ds(32 * (1 - core), 32)], cin.at[s], sC.at[s], rC.at[s], sibling)

    def owner_slot(s, j):
        owner = 8 * (s // 2) + 2 * j + s % 2
        r = (chip + 16 - owner) % 16
        copy = rcopy(gh.at[s, pl.ds(8 * j, 8)], ain.at[r], sA.at[s, j], rA.at[r], chip_dev(owner))
        return r, copy

    def reduce_middle(s):
        arrived(cin.at[s], rC.at[s])
        gh[s] = gf[s, pl.ds(32 * core, 32), :] + cin[s]
        for j in range(4):
            r, copy = owner_slot(s, j)
            pl.when(r != 0)(copy.start)

    own_s, own_rows = 2 * yh + z % 2, pl.ds(8 * (z // 2), 8)

    def peer_copy(r):
        place = fout.at[core, own_s, own_rows]
        return rcopy(res, place, sF.at[r], rF.at[chip], chip_dev((chip + r) % 16))

    def own_work():
        def add(r, total):
            arrived(ain.at[r], rA.at[r])
            return total + ain[r]

        total = lax.fori_loop(1, 16, add, gh[own_s, own_rows, :])
        res[...] = total
        fout[core, own_s, own_rows, :] = total

        def push(r, carry):
            peer_copy(r).start()
            return carry

        lax.fori_loop(1, 16, push, 0)

    def cross_back(g, out, section, saved, partner, bit, peer, ssem, rsem, a, b):
        lower = bit == 0
        kept = []
        for q in range(6):
            cols = pl.ds(128 * q, 128)
            own, other = cross_matrices(factors[section, :, cols], masks, lower)
            zsend[a, :, cols] = hdot_nt(g[:, cols], other).astype(BF16)
            kept.append(own)
        send(zsend.at[a], zsend.at[b], ssem, rsem, peer)
        for q in range(6):
            cols = pl.ds(128 * q, 128)
            field = g[:, cols]
            out[:, cols] = field + hdot_nt(field, kept[q])
            gf[section, pl.ds(32 * bit, 32), cols] = fold_cross(hdot_tn(saved[:, cols], field), masks)
            gf[section, pl.ds(32 * (1 - bit), 32), cols] = fold_cross(hdot_tn(partner[:, cols], field), masks)
        reduce_start(section)
        arrived(zsend.at[b], rsem)
        out[...] += zsend[b].astype(F32)

    def local_back(g, out, section, saved):
        for q in range(6):
            cols = pl.ds(128 * q, 128)
            field = g[:, cols]
            out[:, cols] = field + hdot_nt(field, local_matrix(factors[section, :, cols], masks, section))
        for q in range(6):
            cols = pl.ds(128 * q, 128)
            full = jnp.where(masks[section], hdot_tn(saved[:, cols].astype(F32), g[:, cols]), 0.0)
            if section == 0:
                gf[0, :, cols] = full[:64] + full[64:]
            else:
                gf[1, pl.ds(0, 32), cols] = full[:32] + full[32:64]
                gf[1, pl.ds(32, 32), cols] = full[64:96] + full[96:]
        reduce_start(section)

    cross_back(ga, gb, 3, z3, p3, yl, ypair, sy.at[1], ry.at[1], 4, 5)
    cross_back(gb, ga, 2, z2, p2, x % 2, xpair, sx.at[1], rx.at[1], 6, 7)
    reduce_middle(3)
    reduce_middle(2)
    local_back(ga, gb, 1, z1)
    local_back(gb, grad_tokens, 0, tokens)
    reduce_middle(1)
    reduce_middle(0)
    own_work()
    arrived(px_in.at[0, 2], rP.at[0, 2])
    arrived(px_in.at[1, 1], rP.at[1, 1])
    proj[pl.ds(0, 256), :] = (pbuf[0] + px_in[0, 2].astype(F32) + px_in[1, 1].astype(F32)).astype(BF16)
    arrived(px_in.at[0, 1], rP.at[0, 1])
    arrived(px_in.at[1, 2], rP.at[1, 2])
    proj[pl.ds(256, 256), :] = (pbuf[1] + px_in[0, 1].astype(F32) + px_in[1, 2].astype(F32)).astype(BF16)

    for s in (3, 2, 1, 0):
        for j in range(4):
            owner = 8 * (s // 2) + 2 * j + s % 2

            @pl.when(chip != owner)
            def _():
                arrived(fout.at[core, s, pl.ds(8 * j, 8)], rF.at[owner])
        send(fout.at[core, s], fout.at[core, s], sH.at[s], rH.at[s], sibling)
    for s in range(4):
        arrived(fout.at[1 - core, s], rH.at[s])
        grad_factors[s, pl.ds(0, 32), :] = fout[0, s]
        grad_factors[s, pl.ds(32, 32), :] = fout[1, s]

    for copy in sent:
        copy.wait_send()
    for b in range(2):
        copy = rcopy(rot, R.at[z, slot, core], sys.at[b], yr.at[slot], dev(yh=b, yl=yh))
        pl.when(jnp.logical_not((yh == b) & diagonal))(copy.wait_send)
    for n in range(8):
        rcopy(bsib.at[n], bsib_in.at[n], sB.at[n], rB.at[n], sibling).wait_send()
    rcopy(gsend.at[1], gin.at[0], sG.at[1], rG.at[0], ypair).wait_send()
    pl.when(jnp.logical_not(diagonal))(rcopy(gsend.at[0], gin.at[0], sG.at[0], rG.at[0], ypair).wait_send)

    for s in range(4):
        for j in range(4):
            r, copy = owner_slot(s, j)
            pl.when(r != 0)(copy.wait_send)

    def drain(r, carry):
        peer_copy(r).wait_send()
        return carry

    lax.fori_loop(1, 16, drain, 0)


def per_device(tokens, weight, factors, cotangent):
    V = pltpu.VMEM
    D = pltpu.SemaphoreType.DMA
    field = jax.ShapeDtypeStruct((128, 768), F32)
    vm = pl.BlockSpec(memory_space=pltpu.VMEM)
    hbm = pl.BlockSpec(memory_space=pl.ANY)
    return pl.pallas_call(
        main_kernel,
        out_shape=(jax.ShapeDtypeStruct((512, 896), BF16), field, jax.ShapeDtypeStruct((4, 64, 768), F32)),
        in_specs=[vm, vm, vm, hbm, hbm],
        out_specs=(vm,) * 3,
        scratch_shapes=[
            *[V((128, 768), F32)] * 7,
            V((4, 64, 768), F32),
            V((4, 32, 768), F32),
            V((4, 32, 768), F32),
            V((16, 8, 768), F32),
            V((8, 768), F32),
            V((2, 4, 32, 768), F32),
            V((8, 128, 768), BF16),
            V((128, 768), BF16),
            V((8, 2, 2, 128, 768), BF16),
            V((8, 256, 896), BF16),
            V((768, 896), BF16),
            V((8, 2, 128, 768), BF16),
            V((8, 2, 128, 768), BF16),
            V((8, 2, 128, 768), F32),
            V((7, 128, 768), BF16),
            V((7, 128, 768), BF16),
            V((7, 128, 768), BF16),
            V((7, 128, 768), BF16),
            V((2, 256, 896), F32),
            V((2, 3, 256, 896), BF16),
            V((2, 3, 256, 896), BF16),
            V((2, 128, 768), BF16),
            V((2, 128, 768), BF16),
            D((2,)),
            D((2,)), D((2,)), D((2,)), D((2,)),
            D((6,)), D((6,)), D((3,)), D((3,)),
            D((2,)), D((2,)),
            D((2, 4, 2)), D((2, 4, 2)),
            D((8, 2)), D((8, 2)),
            D((8,)), D((8,)),
            D((2, 7)), D((2, 7)),
            D((2, 3)), D((2, 3)),
            D((2,)), D((2,)),
            D((4,)), D((4,)),
            D((4, 4)), D((16,)),
            D((16,)), D((16,)),
            D((4,)), D((4,)),
        ],
        compiler_params=pltpu.CompilerParams(
            collective_id=0, has_side_effects=True, vmem_limit_bytes=56 * 1024 * 1024
        ),
        name="rotate_project",
    )(tokens, weight, factors, weight, cotangent)


def solution(mesh):
    placed = (P("dp", "tensor"), P("tensor", "dp"), P(None, None, "tensor"), P("tensor", "dp"))
    return jax.shard_map(
        per_device,
        mesh=mesh,
        in_specs=placed,
        out_specs=(P("tensor", "dp"), P("dp", "tensor"), P(None, None, "tensor")),
        check_vma=False,
    )
```

```python
import jax
import jax.numpy as jnp
from jax import lax
from jax.experimental import pallas as pl
from jax.experimental.pallas import tpu as pltpu
from jax.sharding import PartitionSpec as P

HIGH = lax.Precision.HIGHEST
F32 = jnp.float32
BF16 = jnp.bfloat16
MESH = pl.DeviceIdType.MESH
Q = [pl.ds(128 * q, 128) for q in range(6)]
H = [pl.ds(64 * h, 64) for h in range(2)]
M0, M1, OWN2, OTHER2, OWN3, OTHER3 = range(6)


def hdot(a, b, dims=((1,), (0,))):
    return lax.dot_general(a, b, (dims, ((), ())), precision=HIGH, preferred_element_type=F32)


def hdot_nt(a, b):
    return hdot(a, b, ((1,), (1,)))


def hdot_tn(a, b):
    return hdot(a, b, ((0,), (0,)))


def block_masks():
    r = lax.broadcasted_iota(jnp.int32, (128, 128), 0) // 32
    c = lax.broadcasted_iota(jnp.int32, (128, 128), 1) // 32
    return (r // 2 == c // 2, r % 2 == c % 2, r == c)


def fold_cross(full, masks):
    full = jnp.where(masks[2], full, 0.0)
    return full[:32] + full[32:64] + full[64:96] + full[96:]


def main_kernel(
    tokens_hbm, factors_hbm, w_hbm, cot_hbm,
    proj_hbm, grad_tokens_hbm, grad_factors_hbm,
    tokens, factors, proj, grad_factors, w_own, mats, z1, z2, p2, z3, p3, ga, gb, gc, gf, cin, gh, ghb, ain, res, fout,
    zsend, rot, R, cotG, w_oth, bsib, bsib_in, bown, up_out, up_in, dn_out, dn_in,
    pbuf, px_out, px_in, gsend, gin,
    loc_sem, sx, rx, sy, ry, sc, rc, sw, rw, sys, yr, sR, rR, sS, rS, sB, rB, sZ, rZ, sP, rP,
    sG, rG, sC, rC, sA, rA, sF, rF, sH, rH,
):
    dp, tn = lax.axis_index("dp"), lax.axis_index("tensor")
    core, z, yh = dp % 2, dp // 2 % 8, dp // 16
    x, yl = tn % 4, tn // 4
    chip = yh * 8 + z

    def dev(yh=yh, z=z, core=core, yl=yl, x=x):
        return (yh * 16 + z * 2 + core, yl * 4 + x)

    def chip_dev(index):
        return dev(yh=index // 8, z=index % 8)

    xl, xr, xo = (x + 3) % 4, (x + 1) % 4, (x + 2) % 4
    right, left = dev(x=xr), dev(x=xl)
    xpair = dev(x=x + 1 - 2 * (x % 2))
    ypair = dev(yl=1 - yl)
    sibling = dev(core=1 - core)
    above, below = dev(z=(z + 1) % 8), dev(z=(z + 7) % 8)
    diagonal = yh == yl
    off_diagonal = jnp.logical_not(diagonal)

    def rcopy(src, dst, ssem, rsem, to):
        return pltpu.make_async_remote_copy(
            src_ref=src, dst_ref=dst, send_sem=ssem, recv_sem=rsem,
            device_id=to, device_id_type=MESH,
        )

    def send(src, dst, ssem, rsem, to):
        rcopy(src, dst, ssem, rsem, to).start()

    def arrived(dst, rsem):
        rcopy(dst, dst, rsem, rsem, sibling).wait_recv()

    def all_sent(same_bytes, ssem):
        rcopy(same_bytes, same_bytes, ssem, ssem, sibling).wait_send()

    def local(src, dst, n):
        return pltpu.make_async_copy(src, dst, loc_sem.at[n])

    first = [local(tokens_hbm, tokens, 0), local(factors_hbm, factors, 1)]
    for copy in first:
        copy.start()

    barrier = pltpu.get_barrier_semaphore()

    def greet(r, carry):
        pl.semaphore_signal(barrier, inc=1, device_id=chip_dev((chip + r) % 16), device_id_type=MESH)
        return carry

    lax.fori_loop(1, 16, greet, 0)
    for peer in (right, left, ypair, sibling):
        pl.semaphore_signal(barrier, inc=1, device_id=peer, device_id_type=MESH)
    for peer, here in (
        (dev(yh=0, yl=yh), (yh == 0) & diagonal),
        (dev(yh=1, yl=yh), (yh == 1) & diagonal),
        (dev(yh=yl, yl=0), (yl == 0) & diagonal),
        (dev(yh=yl, yl=1), (yl == 1) & diagonal),
    ):
        @pl.when(jnp.logical_not(here))
        def _():
            pl.semaphore_signal(barrier, inc=1, device_id=peer, device_id_type=MESH)

    own_cot = [local(cot_hbm.at[pl.ds(256 * i, 256)], cotG.at[2 * x + i], 2 + i) for i in range(2)]
    own_w = local(w_hbm, w_own, 4)
    own_w.start()
    for copy in own_cot:
        copy.start()
    for copy in first:
        copy.wait()

    masks = block_masks()
    for q, cols in enumerate(Q):
        c0, c1 = factors[0, :, cols], factors[1, :, cols]
        mats[M0, q] = jnp.where(masks[0], jnp.concatenate([c0, c0], 0), 0.0)
        mats[M1, q] = jnp.where(
            masks[1], jnp.concatenate([c1[:32], c1[:32], c1[32:], c1[32:]], 0), 0.0
        )
        for section, bit, own in ((2, x % 2, OWN2), (3, yl, OWN3)):
            for part, place in ((bit, own), (1 - bit, own + 1)):
                coeffs = factors[section, pl.ds(32 * part, 32), cols]
                mats[place, q] = jnp.where(masks[2], jnp.concatenate([coeffs] * 4, 0), 0.0)
    for q, cols in enumerate(Q):
        field = tokens[:, cols].astype(F32)
        field = field + hdot(field, mats[M0, q])
        z1[:, cols] = field
        field = field + hdot(field, mats[M1, q])
        z2[:, cols] = field
        zsend[0, :, cols] = field.astype(BF16)

    pl.semaphore_wait(barrier, 23 - 2 * diagonal.astype(jnp.int32))

    def send_w(i):
        rows = pl.ds(128 * i, 128)
        send(w_hbm.at[rows], w_oth.at[rows], sw, rw, ypair)

    for h in range(2):
        send(zsend.at[0, H[h]], zsend.at[2, H[h]], sx, rx.at[h], xpair)
    send_w(0)
    for h in range(2):
        arrived(zsend.at[2, H[h]], rx.at[h])
        for q, cols in enumerate(Q):
            theirs = zsend[2, H[h], cols].astype(F32)
            p2[H[h], cols] = theirs
            field = z2[H[h], cols]
            field = field + hdot(field, mats[OWN2, q]) + hdot(theirs, mats[OTHER2, q])
            z3[H[h], cols] = field
            zsend[1, H[h], cols] = field.astype(BF16)
        send(zsend.at[1, H[h]], zsend.at[3, H[h]], sy, ry.at[h], ypair)

    for i, to in ((0, right), (1, left), (1, right), (0, left)):
        n = i + (0 if to is right else 2)
        send(cot_hbm.at[pl.ds(256 * i, 256)], cotG.at[2 * x + i], sc, rc.at[n], to)

    slot = (yl + yh) % 2

    def to_holder(b, h):
        src = rot.at[H[h]]
        dst = R.at[z, slot, core, H[h]]
        return rcopy(src, dst, sys.at[b], yr.at[slot, h], dev(yh=b, yl=yh))

    for h in range(2):
        arrived(zsend.at[3, H[h]], ry.at[h])
        for q, cols in enumerate(Q):
            theirs = zsend[3, H[h], cols].astype(F32)
            p3[H[h], cols] = theirs
            field = z3[H[h], cols]
            field = field + hdot(field, mats[OWN3, q]) + hdot(theirs, mats[OTHER3, q])
            rot[H[h], cols] = field.astype(BF16)
        for b in range(2):
            pl.when(jnp.logical_not((yh == b) & diagonal))(to_holder(b, h).start)

    @pl.when(diagonal)
    def _():
        R[z, 0, core] = rot[...]

    def spread(zz, s, up, down, k):
        block = R.at[zz, s, core]
        if up:
            send(block, block, sR.at[0], rR.at[0, k, s], above)
        if down:
            send(block, block, sR.at[1], rR.at[1, k, s], below)
        send(block, block, sS, rS, sibling)

    @pl.when(off_diagonal)
    def _():
        for h in range(2):
            arrived(R.at[z, 0, core, H[h]], yr.at[0, h])
    spread(z, 0, True, True, 0)
    for h in range(2):
        arrived(R.at[z, 1, core, H[h]], yr.at[1, h])
    spread(z, 1, True, True, 0)
    for i in range(1, 6):
        send_w(i)

    arrived(cotG.at[2 * xl], rc.at[0])
    send(cotG.at[2 * xl], cotG.at[2 * xl], sc, rc.at[4], right)
    arrived(cotG.at[2 * xr + 1], rc.at[3])
    send(cotG.at[2 * xr + 1], cotG.at[2 * xr + 1], sc, rc.at[5], left)

    def step(k):
        lo, hi = (z + 8 - k) % 8, (z + k) % 8
        for s in range(2):
            arrived(R.at[lo, s, core], rR.at[0, k - 1, s])
            spread(lo, s, k < 3 or s == 0, False, k)
            arrived(R.at[hi, s, core], rR.at[1, k - 1, s])
            spread(hi, s, False, k < 3 or s == 1, k)

    def sib_copy(zz, s):
        return rcopy(bsib.at[zz, s], bsib_in.at[zz, s], sB, rB.at[zz, s], sibling)

    def back_unit(xb, s):
        rows = cotG[pl.ds(2 * xb, 2)].reshape(512, 896)
        w = w_oth if s else w_own
        part = lax.dot_general(rows, w[...], (((1,), (1,)), ((), ())), preferred_element_type=F32)
        for c in range(2):
            @pl.when(core == c)
            def _():
                for i in range(2):
                    first, second = 256 * i + 128 * c, 256 * i + 128 * (1 - c)
                    bown[2 * xb + i, s] = part[first:first + 128]
                    bsib[2 * xb + i, s] = part[second:second + 128].astype(BF16)
        for i in range(2):
            sib_copy(2 * xb + i, s).start()

    for copy in own_cot:
        copy.wait()
    own_w.wait()
    back_unit(x, 0)
    step(1)
    arrived(cotG.at[2 * xl + 1], rc.at[1])
    back_unit(xl, 0)
    arrived(cotG.at[2 * xr], rc.at[2])
    back_unit(xr, 0)
    step(2)
    arrived(cotG.at[2 * xo], rc.at[4])
    arrived(cotG.at[2 * xo + 1], rc.at[5])
    back_unit(xo, 0)
    step(3)

    def back_ready(zz, s):
        arrived(bsib_in.at[zz, s], rB.at[zz, s])

    def own_back(zz, s, rows=slice(None)):
        return bown[zz, s, rows] + bsib_in[zz, s, rows].astype(F32)

    def ring_send(direction, n, zz, s, incoming, h=None):
        out, into = (up_out, up_in) if direction == 0 else (dn_out, dn_in)
        rows = slice(None) if h is None else H[h]
        value = own_back(zz, s, rows)
        if incoming is not None:
            if not h:
                arrived(into.at[incoming], rZ.at[direction, incoming, 0])
            value = value + into[incoming, rows].astype(F32)
        out[n, rows] = value.astype(BF16)
        src, dst = (out.at[n], into.at[n]) if h is None else (out.at[n, rows], into.at[n, rows])
        send(src, dst, sZ.at[direction], rZ.at[direction, n, h or 0], below if direction else above)

    def z_at(k):
        return (z + 8 + k) % 8

    back_ready(z_at(4), 0)
    ring_send(0, 0, z_at(4), 0, None)
    back_ready(z_at(-3), 0)
    ring_send(1, 1, z_at(-3), 0, None)

    arrived(w_oth, rw)
    far = z_at(4) // 2
    turn = 2 * (z % 2) - 1
    back_unit(far, 1)
    back_ready(z_at(4), 1)
    ring_send(1, 0, z_at(4), 1, None)
    back_unit((far + 4 + turn) % 4, 1)
    back_ready(z_at(3), 1)
    ring_send(0, 1, z_at(3), 1, None)

    zf = z_at(4)
    arrived(R.at[zf, 0, core], rR.at[0, 3, 0])
    spread(zf, 0, False, False, 4)
    arrived(R.at[zf, 1, core], rR.at[1, 3, 1])
    spread(zf, 1, False, False, 4)

    arrived(bsib, rS)

    def product(zz):
        return jnp.dot(R[zz, 0].reshape(256, 768), w_own[...], preferred_element_type=F32) + jnp.dot(
            R[zz, 1].reshape(256, 768), w_oth[...], preferred_element_type=F32
        )

    def px_send(direction, n, zz, incoming):
        value = product(zz)
        if incoming is not None:
            arrived(px_in.at[direction, incoming], rP.at[direction, incoming])
            value = value + px_in[direction, incoming].astype(F32)
        px_out[direction, n] = value.astype(BF16)
        send(px_out.at[direction, n], px_in.at[direction, n], sP, rP.at[direction, n], left if direction else right)

    px_send(0, 0, 2 * xo, None)
    px_send(1, 0, 2 * xo + 1, None)
    back_ready(z_at(3), 0)
    back_ready(z_at(-3), 1)
    ring_send(0, 2, z_at(3), 0, 0)
    ring_send(1, 2, z_at(-3), 1, 0)
    back_unit((far + 4 - turn) % 4, 1)
    back_unit((far + 2) % 4, 1)
    back_ready(z_at(2), 1)
    ring_send(0, 3, z_at(2), 1, 1)
    back_ready(z_at(-2), 0)
    ring_send(1, 3, z_at(-2), 0, 1)
    px_send(0, 1, 2 * xr + 1, None)
    px_send(1, 1, 2 * xl, None)
    back_ready(z_at(2), 0)
    ring_send(0, 4, z_at(2), 0, 2)
    back_ready(z_at(-2), 1)
    ring_send(1, 4, z_at(-2), 1, 2)
    back_ready(z_at(1), 1)
    back_ready(z_at(-1), 0)
    back_ready(z_at(1), 0)
    back_ready(z_at(-1), 1)
    for h in range(2):
        ring_send(0, 5, z_at(1), 1, 3, h)
        ring_send(1, 5, z_at(-1), 0, 3, h)
        ring_send(0, 6, z_at(1), 0, 4, h)
        ring_send(1, 6, z_at(-1), 1, 4, h)
    px_send(0, 2, 2 * xr, 0)
    px_send(1, 2, 2 * xl + 1, 0)
    back_ready(z, 0)
    back_ready(z, 1)
    pbuf[0] = product(2 * x)
    pbuf[1] = product(2 * x + 1)

    def to_owner(s, h):
        return rcopy(gsend.at[s, H[h]], gin.at[yh, H[h]], sG.at[s], rG.at[yh, h], dev(yh=yl, yl=(yl + s) % 2))

    for h in range(2):
        rows = H[h]
        for s, nu, nd in ((1, 5, 6), (0, 6, 5)):
            arrived(up_in.at[nu, rows], rZ.at[0, nu, h])
            arrived(dn_in.at[nd, rows], rZ.at[1, nd, h])
            total = own_back(z, s, rows) + up_in[nu, rows].astype(F32) + dn_in[nd, rows].astype(F32)
            gsend[s, rows] = total.astype(BF16)
            if s == 1:
                to_owner(s, h).start()
            else:
                pl.when(off_diagonal)(to_owner(s, h).start)

                @pl.when(diagonal)
                def _():
                    gin[yh, rows] = gsend[0, rows]

    def reduce_start(s):
        send(gf.at[s, pl.ds(32 * (1 - core), 32)], cin.at[s], sC, rC.at[s], sibling)

    def piece(j):
        return (pl.ds(16 * (j // 2), 16), pl.ds(384 * (j % 2), 384))

    def owner_of(s, j):
        return 8 * (j % 2) + 4 * (j // 2) + s

    def owner_copy(s, j):
        owner = owner_of(s, j)
        r = (chip + 16 - owner) % 16
        src = ghb.at[s, piece(j)[0], piece(j)[1]]
        return r, rcopy(src, ain.at[(r + 15) % 16], sA, rA, chip_dev(owner))

    def reduce_middle(s):
        arrived(cin.at[s], rC.at[s])
        gh[s] = gf[s, pl.ds(32 * core, 32), :] + cin[s]
        ghb[s] = gh[s].astype(BF16)
        for j in range(4):
            r, copy = owner_copy(s, j)
            pl.when(r != 0)(copy.start)

    own_s = z % 4
    own_rows, own_cols = pl.ds(16 * (z // 4), 16), pl.ds(384 * yh, 384)

    def peer_copy(r):
        place = fout.at[core, own_s, own_rows, own_cols]
        return rcopy(res, place, sF, rF.at[own_s], chip_dev((chip + r) % 16))

    def own_work():
        arrived(ain.at[pl.ds(0, 15)], rA)

        def add(r, total):
            return total + ain[r - 1].astype(F32)

        total = lax.fori_loop(1, 16, add, gh[own_s, own_rows, own_cols])
        res[...] = total.astype(BF16)
        fout[core, own_s, own_rows, own_cols] = res[...]

        def push(r, carry):
            peer_copy(r).start()
            return carry

        lax.fori_loop(1, 16, push, 0)

    def cross_out(g, h, other, a, ssem, rsem, peer):
        for q, cols in enumerate(Q):
            zsend[a, H[h], cols] = hdot_nt(g[H[h], cols], mats[other, q]).astype(BF16)
        send(zsend.at[a, H[h]], zsend.at[a + 1, H[h]], ssem, rsem, peer)

    def cross_kept(g, out, section, own, saved, partner, bit):
        for q, cols in enumerate(Q):
            field = g[:, cols]
            out[:, cols] = field + hdot_nt(field, mats[own, q])
            gf[section, pl.ds(32 * bit, 32), cols] = fold_cross(hdot_tn(saved[:, cols], field), masks)
            gf[section, pl.ds(32 * (1 - bit), 32), cols] = fold_cross(hdot_tn(partner[:, cols], field), masks)
        reduce_start(section)

    def cross_in(out, h, a, rsem):
        arrived(zsend.at[a + 1, H[h]], rsem)
        out[H[h]] += zsend[a + 1, H[h]].astype(F32)

    def local_back(g, out, section, saved):
        for q, cols in enumerate(Q):
            field = g[:, cols]
            out[:, cols] = field + hdot_nt(field, mats[section, q])
            full = jnp.where(masks[section], hdot_tn(saved[:, cols].astype(F32), field), 0.0)
            if section == 0:
                gf[0, :, cols] = full[:64] + full[64:]
            else:
                gf[1, pl.ds(0, 32), cols] = full[:32] + full[32:64]
                gf[1, pl.ds(32, 32), cols] = full[64:96] + full[96:]
        reduce_start(section)

    for h in range(2):
        for a in range(2):
            @pl.when(jnp.logical_not((yh == a) & diagonal))
            def _():
                arrived(gin.at[a, H[h]], rG.at[a, h])
        ga[H[h]] = gin[0, H[h]].astype(F32) + gin[1, H[h]].astype(F32)
        cross_out(ga, h, OTHER3, 4, sy, ry.at[2 + h], ypair)
    cross_kept(ga, gb, 3, OWN3, z3, p3, yl)
    for h in range(2):
        cross_in(gb, h, 4, ry.at[2 + h])
        cross_out(gb, h, OTHER2, 6, sx, rx.at[2 + h], xpair)
    cross_kept(gb, gc, 2, OWN2, z2, p2, x % 2)
    for h in range(2):
        cross_in(gc, h, 6, rx.at[2 + h])
    reduce_middle(3)
    local_back(gc, gb, 1, z1)
    local_back(gb, ga, 0, tokens)
    grad_tokens_out = local(ga, grad_tokens_hbm, 5)
    grad_tokens_out.start()
    reduce_middle(2)
    reduce_middle(1)
    reduce_middle(0)
    pl.when(own_s >= 2)(own_work)
    for i, nu, nd in ((0, 2, 1), (1, 1, 2)):
        arrived(px_in.at[0, nu], rP.at[0, nu])
        arrived(px_in.at[1, nd], rP.at[1, nd])
        total = pbuf[i] + px_in[0, nu].astype(F32) + px_in[1, nd].astype(F32)
        proj[pl.ds(256 * i, 256), :] = total.astype(BF16)

    proj_out = local(proj, proj_hbm, 6)
    proj_out.start()
    pl.when(own_s < 2)(own_work)
    for s in (3, 2, 1, 0):
        @pl.when(own_s != s)
        def _():
            arrived(ain.at[pl.ds(0, 4)], rF.at[s])

        @pl.when(own_s == s)
        def _():
            arrived(ain.at[pl.ds(0, 3)], rF.at[s])

        send(fout.at[core, s], fout.at[core, s], sH, rH.at[s], sibling)
        grad_factors[s, pl.ds(32 * core, 32), :] = fout[core, s].astype(F32)
    factors_out = [local(grad_factors.at[s], grad_factors_hbm.at[s], 7 + s) for s in range(4)]
    for s in (3, 2, 1, 0):
        arrived(fout.at[1 - core, s], rH.at[s])
        grad_factors[s, pl.ds(32 - 32 * core, 32), :] = fout[1 - core, s].astype(F32)
        factors_out[s].start()

    for copy in (grad_tokens_out, proj_out, *factors_out):
        copy.wait()
    all_sent(zsend.at[pl.ds(0, 2)], sx)
    all_sent(zsend.at[pl.ds(0, 2)], sy)
    all_sent(px_out, sc)
    all_sent(w_oth, sw)
    for b in range(2):
        pl.when(jnp.logical_not((yh == b) & diagonal))(lambda: all_sent(rot, sys.at[b]))
        all_sent(up_out, sR.at[b])
        all_sent(up_out, sZ.at[b])
    all_sent(bsib, sS)
    all_sent(bsib, sB)
    all_sent(px_out, sP)
    pl.when(off_diagonal)(lambda: all_sent(rot, sG.at[0]))
    all_sent(rot, sG.at[1])
    all_sent(cin, sC)
    all_sent(ain.at[pl.ds(0, 15)], sA)
    all_sent(ain.at[pl.ds(0, 15)], sF)
    all_sent(fout.at[0], sH)


def per_device(tokens, weight, factors, cotangent):
    V = pltpu.VMEM
    D = pltpu.SemaphoreType.DMA
    shapes = (
        jax.ShapeDtypeStruct((512, 896), BF16),
        jax.ShapeDtypeStruct((128, 768), F32),
        jax.ShapeDtypeStruct((4, 64, 768), F32),
    )
    hbm = pl.BlockSpec(memory_space=pl.ANY)
    return pl.pallas_call(
        main_kernel,
        out_shape=shapes,
        in_specs=[hbm] * 4,
        out_specs=(hbm,) * 3,
        scratch_shapes=[
            V((128, 768), BF16),
            V((4, 64, 768), F32),
            V((512, 896), BF16),
            V((4, 64, 768), F32),
            V((768, 896), BF16),
            V((6, 6, 128, 128), F32),
            *[V((128, 768), F32)] * 8,
            V((4, 64, 768), F32),
            V((4, 32, 768), F32),
            V((4, 32, 768), F32),
            V((4, 32, 768), BF16),
            V((16, 16, 384), BF16),
            V((16, 384), BF16),
            V((2, 4, 32, 768), BF16),
            V((8, 128, 768), BF16),
            V((128, 768), BF16),
            V((8, 2, 2, 128, 768), BF16),
            V((8, 256, 896), BF16),
            V((768, 896), BF16),
            V((8, 2, 128, 768), BF16),
            V((8, 2, 128, 768), BF16),
            V((8, 2, 128, 768), F32),
            *[V((7, 128, 768), BF16)] * 4,
            V((2, 256, 896), F32),
            V((2, 3, 256, 896), BF16),
            V((2, 3, 256, 896), BF16),
            V((2, 128, 768), BF16),
            V((2, 128, 768), BF16),
            D((11,)),
            D, D((4,)), D, D((4,)),
            D, D((6,)), D, D,
            D((2,)), D((2, 2)),
            D((2,)), D((2, 4, 2)),
            D, D,
            D, D((8, 2)),
            D((2,)), D((2, 7, 2)),
            D, D((2, 3)),
            D((2,)), D((2, 2)),
            D, D((4,)),
            D, D,
            D, D((4,)),
            D, D((4,)),
        ],
        compiler_params=pltpu.CompilerParams(
            collective_id=0, has_side_effects=True, vmem_limit_bytes=56 * 1024 * 1024
        ),
        name="rotate_project",
    )(tokens, factors, weight, cotangent)


def solution(mesh):
    placed = (P("dp", "tensor"), P("tensor", "dp"), P(None, None, "tensor"), P("tensor", "dp"))
    return jax.shard_map(
        per_device,
        mesh=mesh,
        in_specs=placed,
        out_specs=(P("tensor", "dp"), P("dp", "tensor"), P(None, None, "tensor")),
        check_vma=False,
    )
```

```python
import jax
import jax.numpy as jnp
from jax import lax
from jax.experimental import pallas as pl
from jax.experimental.pallas import tpu as pltpu
from jax.sharding import PartitionSpec as P

HIGH = lax.Precision.HIGHEST
F32 = jnp.float32
BF16 = jnp.bfloat16
MESH = pl.DeviceIdType.MESH
Q = [pl.ds(128 * q, 128) for q in range(6)]
H = [pl.ds(64 * h, 64) for h in range(2)]
M0, M1, OWN2, OTHER2, OWN3, OTHER3 = range(6)


def hdot(a, b, dims=((1,), (0,))):
    return lax.dot_general(a, b, (dims, ((), ())), precision=HIGH, preferred_element_type=F32)


def hdot_nt(a, b):
    return hdot(a, b, ((1,), (1,)))


def hdot_tn(a, b):
    return hdot(a, b, ((0,), (0,)))


def block_masks():
    r = lax.broadcasted_iota(jnp.int32, (128, 128), 0) // 32
    c = lax.broadcasted_iota(jnp.int32, (128, 128), 1) // 32
    return (r // 2 == c // 2, r % 2 == c % 2, r == c)


def fold_cross(full, masks):
    full = jnp.where(masks[2], full, 0.0)
    return full[:32] + full[32:64] + full[64:96] + full[96:]


def main_kernel(
    tokens_hbm, factors_hbm, w_hbm, cot_hbm,
    proj_hbm, grad_tokens_hbm, grad_factors_hbm,
    tokens, factors, proj, grad_factors, w_own, mats, z1, z2, p2, z3, p3, ga, gb, gc, gf, cin, gh, ghb, ain, res, fout,
    zsend, rot, R, cotG, w_oth, bsib, bsib_in, bown, up_out, up_in, dn_out, dn_in,
    pbuf, px_out, px_in, gsend, gin,
    loc_sem, sx, rx, sy, ry, sc, rc, sw, rw, sys, yr, sR, rR, sS, rS, sB, rB, sZ, rZ, sP, rP,
    sG, rG, sC, rC, sA, rA, sF, rF, sH, rH,
):
    dp, tn = lax.axis_index("dp"), lax.axis_index("tensor")
    core, z, yh = dp % 2, dp // 2 % 8, dp // 16
    x, yl = tn % 4, tn // 4
    chip = yh * 8 + z

    def dev(yh=yh, z=z, core=core, yl=yl, x=x):
        return (yh * 16 + z * 2 + core, yl * 4 + x)

    def chip_dev(index):
        return dev(yh=index // 8, z=index % 8)

    xl, xr, xo = (x + 3) % 4, (x + 1) % 4, (x + 2) % 4
    right, left = dev(x=xr), dev(x=xl)
    xpair = dev(x=x + 1 - 2 * (x % 2))
    ypair = dev(yl=1 - yl)
    sibling = dev(core=1 - core)
    above, below = dev(z=(z + 1) % 8), dev(z=(z + 7) % 8)
    diagonal = yh == yl
    off_diagonal = jnp.logical_not(diagonal)

    def rcopy(src, dst, ssem, rsem, to):
        return pltpu.make_async_remote_copy(
            src_ref=src, dst_ref=dst, send_sem=ssem, recv_sem=rsem,
            device_id=to, device_id_type=MESH,
        )

    def send(src, dst, ssem, rsem, to):
        rcopy(src, dst, ssem, rsem, to).start()

    def arrived(dst, rsem):
        rcopy(dst, dst, rsem, rsem, sibling).wait_recv()

    def all_sent(same_bytes, ssem):
        rcopy(same_bytes, same_bytes, ssem, ssem, sibling).wait_send()

    def local(src, dst, n):
        return pltpu.make_async_copy(src, dst, loc_sem.at[n])

    first = [local(tokens_hbm, tokens, 0), local(factors_hbm, factors, 1)]
    for copy in first:
        copy.start()

    barrier = pltpu.get_barrier_semaphore()

    def greet(r, carry):
        pl.semaphore_signal(barrier, inc=1, device_id=chip_dev((chip + r) % 16), device_id_type=MESH)
        return carry

    lax.fori_loop(1, 16, greet, 0)
    for peer in (right, left, ypair, sibling):
        pl.semaphore_signal(barrier, inc=1, device_id=peer, device_id_type=MESH)
    for peer, here in (
        (dev(yh=0, yl=yh), (yh == 0) & diagonal),
        (dev(yh=1, yl=yh), (yh == 1) & diagonal),
        (dev(yh=yl, yl=0), (yl == 0) & diagonal),
        (dev(yh=yl, yl=1), (yl == 1) & diagonal),
    ):
        @pl.when(jnp.logical_not(here))
        def _():
            pl.semaphore_signal(barrier, inc=1, device_id=peer, device_id_type=MESH)

    own_cot = [local(cot_hbm.at[pl.ds(256 * i, 256)], cotG.at[2 * x + i], 2 + i) for i in range(2)]
    own_w = local(w_hbm, w_own, 4)
    own_w.start()
    for copy in own_cot:
        copy.start()
    for copy in first:
        copy.wait()

    masks = block_masks()
    for q, cols in enumerate(Q):
        c0, c1 = factors[0, :, cols], factors[1, :, cols]
        mats[M0, q] = jnp.where(masks[0], jnp.concatenate([c0, c0], 0), 0.0)
        mats[M1, q] = jnp.where(
            masks[1], jnp.concatenate([c1[:32], c1[:32], c1[32:], c1[32:]], 0), 0.0
        )
        for section, bit, own in ((2, x % 2, OWN2), (3, yl, OWN3)):
            for part, place in ((bit, own), (1 - bit, own + 1)):
                coeffs = factors[section, pl.ds(32 * part, 32), cols]
                mats[place, q] = jnp.where(masks[2], jnp.concatenate([coeffs] * 4, 0), 0.0)
    for q, cols in enumerate(Q):
        field = tokens[:, cols].astype(F32)
        field = field + hdot(field, mats[M0, q])
        z1[:, cols] = field
        field = field + hdot(field, mats[M1, q])
        z2[:, cols] = field
        zsend[0, :, cols] = field.astype(BF16)

    pl.semaphore_wait(barrier, 23 - 2 * diagonal.astype(jnp.int32))

    def send_w(i):
        rows = pl.ds(128 * i, 128)
        send(w_hbm.at[rows], w_oth.at[rows], sw, rw, ypair)

    for h in range(2):
        send(zsend.at[0, H[h]], zsend.at[2, H[h]], sx, rx.at[h], xpair)
    for i, to in ((0, right), (1, left), (1, right), (0, left)):
        n = i + (0 if to is right else 2)
        send(cot_hbm.at[pl.ds(256 * i, 256)], cotG.at[2 * x + i], sc, rc.at[n], to)
    send_w(0)
    for h in range(2):
        arrived(zsend.at[2, H[h]], rx.at[h])
        for q, cols in enumerate(Q):
            theirs = zsend[2, H[h], cols].astype(F32)
            p2[H[h], cols] = theirs
            field = z2[H[h], cols]
            field = field + hdot(field, mats[OWN2, q]) + hdot(theirs, mats[OTHER2, q])
            z3[H[h], cols] = field
            zsend[1, H[h], cols] = field.astype(BF16)
        send(zsend.at[1, H[h]], zsend.at[3, H[h]], sy, ry.at[h], ypair)

    slot = (yl + yh) % 2

    def to_holder(b, h):
        src = rot.at[H[h]]
        dst = R.at[z, slot, core, H[h]]
        return rcopy(src, dst, sys.at[b], yr.at[slot, h], dev(yh=b, yl=yh))

    for h in range(2):
        arrived(zsend.at[3, H[h]], ry.at[h])
        for q, cols in enumerate(Q):
            theirs = zsend[3, H[h], cols].astype(F32)
            p3[H[h], cols] = theirs
            field = z3[H[h], cols]
            field = field + hdot(field, mats[OWN3, q]) + hdot(theirs, mats[OTHER3, q])
            rot[H[h], cols] = field.astype(BF16)
        for b in range(2):
            pl.when(jnp.logical_not((yh == b) & diagonal))(to_holder(b, h).start)

    @pl.when(diagonal)
    def _():
        R[z, 0, core] = rot[...]

    def spread(zz, s, up, down, k):
        block = R.at[zz, s, core]
        if up:
            send(block, block, sR.at[0], rR.at[0, k, s], above)
        if down:
            send(block, block, sR.at[1], rR.at[1, k, s], below)
        send(block, block, sS, rS.at[int(k > 2)], sibling)

    @pl.when(off_diagonal)
    def _():
        for h in range(2):
            arrived(R.at[z, 0, core, H[h]], yr.at[0, h])
    spread(z, 0, True, True, 0)
    for h in range(2):
        arrived(R.at[z, 1, core, H[h]], yr.at[1, h])
    spread(z, 1, True, True, 0)
    for i in range(1, 6):
        send_w(i)

    arrived(cotG.at[2 * xl], rc.at[0])
    send(cotG.at[2 * xl], cotG.at[2 * xl], sc, rc.at[4], right)
    arrived(cotG.at[2 * xr + 1], rc.at[3])
    send(cotG.at[2 * xr + 1], cotG.at[2 * xr + 1], sc, rc.at[5], left)

    def step(k, onward):
        lo, hi = (z + 8 - k) % 8, (z + k) % 8
        for s in range(2):
            arrived(R.at[lo, s, core], rR.at[0, k - 1, s])
            spread(lo, s, onward or s == 0, False, k)
            arrived(R.at[hi, s, core], rR.at[1, k - 1, s])
            spread(hi, s, False, onward or s == 0, k)

    def sib_copy(zz, s):
        return rcopy(bsib.at[zz, s], bsib_in.at[zz, s], sB, rB.at[zz, s], sibling)

    def back_unit(xb, s):
        rows = cotG[pl.ds(2 * xb, 2)].reshape(512, 896)
        w = w_oth if s else w_own
        part = lax.dot_general(rows, w[...], (((1,), (1,)), ((), ())), preferred_element_type=F32)
        for c in range(2):
            @pl.when(core == c)
            def _():
                for i in range(2):
                    first, second = 256 * i + 128 * c, 256 * i + 128 * (1 - c)
                    bown[2 * xb + i, s] = part[first:first + 128]
                    bsib[2 * xb + i, s] = part[second:second + 128].astype(BF16)
        for i in range(2):
            sib_copy(2 * xb + i, s).start()

    for copy in own_cot:
        copy.wait()
    own_w.wait()
    back_unit(x, 0)
    step(1, True)
    arrived(cotG.at[2 * xl + 1], rc.at[1])
    back_unit(xl, 0)
    arrived(cotG.at[2 * xr], rc.at[2])
    back_unit(xr, 0)
    step(2, False)
    arrived(cotG.at[2 * xo], rc.at[4])
    arrived(cotG.at[2 * xo + 1], rc.at[5])
    back_unit(xo, 0)

    def z_at(k):
        return (z + 8 + k) % 8

    def back_ready(s, *places):
        for k in places:
            arrived(bsib_in.at[z_at(k), s], rB.at[z_at(k), s])

    def own_back(zz, s, rows):
        return bown[zz, s, rows] + bsib_in[zz, s, rows].astype(F32)

    def ring_send(s, n):
        for direction in range(2):
            out, into = (dn_out, dn_in) if direction else (up_out, up_in)
            distance = 4 - (n + 1) // 2
            h = direction if n % 2 == 0 else 1 - direction
            value = own_back(z_at(-distance if direction else distance), s, H[h])
            if n >= 2:
                arrived(into.at[7 * s + n - 2], rZ.at[direction, 7 * s + n - 2])
                value = value + into[7 * s + n - 2].astype(F32)
            m = 7 * s + n
            out[m] = value.astype(BF16)
            send(out.at[m], into.at[m], sZ.at[direction], rZ.at[direction, m], below if direction else above)

    def to_owner(s, h):
        return rcopy(gsend.at[s, H[h]], gin.at[yh, H[h]], sG.at[s], rG.at[yh, h], dev(yh=yl, yl=(yl + s) % 2))

    def ring_end(s):
        for h in (1, 0):
            nu, nd = 7 * s + 6 - h, 7 * s + 5 + h
            arrived(up_in.at[nu], rZ.at[0, nu])
            arrived(dn_in.at[nd], rZ.at[1, nd])
            total = own_back(z, s, H[h]) + up_in[nu].astype(F32) + dn_in[nd].astype(F32)
            gsend[s, H[h]] = total.astype(BF16)
            if s == 1:
                to_owner(s, h).start()
            else:
                pl.when(off_diagonal)(to_owner(s, h).start)

                @pl.when(diagonal)
                def _():
                    gin[yh, H[h]] = gsend[0, H[h]]

    def product(zz):
        return jnp.dot(R[zz, 0].reshape(256, 768), w_own[...], preferred_element_type=F32) + jnp.dot(
            R[zz, 1].reshape(256, 768), w_oth[...], preferred_element_type=F32
        )

    def in_phase(zz, late):
        away = (zz - z + 8) % 8
        return ((away >= 3) & (away <= 5)) == late

    def px_send(late, n, after_far=None):
        for direction in range(2):
            zz = ((2 * xo + 1, 2 * xr, 2 * xr + 1), (2 * xo, 2 * xl + 1, 2 * xl))[direction][n]
            now = in_phase(zz, late)
            if after_far is not None:
                now = now & in_phase(2 * xo + 1 - direction, after_far)

            @pl.when(now)
            def _():
                value = product(zz)
                if n == 2:
                    arrived(px_in.at[direction, 0], rP.at[direction, 0])
                    value = value + px_in[direction, 0].astype(F32)
                px_out[direction, n] = value.astype(BF16)
                send(
                    px_out.at[direction, n], px_in.at[direction, n], sP, rP.at[direction, n],
                    left if direction else right,
                )

    def px_own(late):
        for i in range(2):
            @pl.when(in_phase(2 * x + i, late))
            def _():
                pbuf[i] = product(2 * x + i)

    def third_step(s):
        lo, hi = z_at(-3), z_at(3)
        arrived(R.at[lo, s, core], rR.at[0, 2, s])
        spread(lo, s, False, False, 3)
        arrived(R.at[hi, s, core], rR.at[1, 2, s])
        spread(hi, s, False, s == 1, 3)

    def last_step():
        zf = z_at(4)
        for s in range(2):
            arrived(R.at[zf, s, core], rR.at[s, 3, s])
            spread(zf, s, False, False, 4)

    back_ready(0, 4, 3, -3)
    ring_send(0, 0)
    ring_send(0, 1)
    back_ready(0, 2, -2, 1, -1, 0)
    ring_send(0, 2)
    ring_send(0, 3)
    arrived(w_oth, rw)
    far = z_at(4) // 2
    turn = 2 * (z % 2) - 1
    back_unit(far, 1)
    ring_send(0, 4)
    arrived(R.at[pl.ds(0, 5), :, 0], rS.at[0])
    px_send(False, 0)
    ring_send(0, 5)
    back_unit((far + 4 + turn) % 4, 1)
    ring_send(0, 6)
    back_ready(1, 4, 3, -3)
    ring_send(1, 0)
    ring_send(1, 1)
    back_unit((far + 4 - turn) % 4, 1)
    third_step(0)
    back_unit((far + 2) % 4, 1)
    ring_send(1, 2)
    ring_end(0)
    back_ready(1, 2, -2)
    ring_send(1, 3)
    px_send(False, 1)
    ring_send(1, 4)
    back_ready(1, 1, -1, 0)
    ring_send(1, 5)
    px_own(False)
    ring_send(1, 6)
    held = ((z_at(-2), 1, 0, 2, above), (z_at(2), 1, 1, 2, below), (z_at(-3), 0, 0, 3, above))
    for zz, s, direction, k, to in held:
        block = R.at[zz, s, core]
        send(block, block, sR.at[direction], rR.at[direction, k, s], to)
    px_send(False, 2)
    ring_end(1)
    third_step(1)

    def reduce_start(s):
        send(gf.at[s, pl.ds(32 * (1 - core), 32)], cin.at[s], sC, rC.at[s], sibling)

    def piece(j):
        return (pl.ds(16 * (j // 2), 16), pl.ds(384 * (j % 2), 384))

    def owner_of(s, j):
        return 8 * (j % 2) + 4 * (j // 2) + s

    def owner_copy(s, j):
        owner = owner_of(s, j)
        r = (chip + 16 - owner) % 16
        src = ghb.at[s, piece(j)[0], piece(j)[1]]
        return r, rcopy(src, ain.at[(r + 15) % 16], sA, rA, chip_dev(owner))

    def reduce_middle(s):
        arrived(cin.at[s], rC.at[s])
        gh[s] = gf[s, pl.ds(32 * core, 32), :] + cin[s]
        ghb[s] = gh[s].astype(BF16)
        for j in range(4):
            r, copy = owner_copy(s, j)
            pl.when(r != 0)(copy.start)

    own_s = z % 4
    own_rows, own_cols = pl.ds(16 * (z // 4), 16), pl.ds(384 * yh, 384)

    def peer_copy(r):
        place = fout.at[core, own_s, own_rows, own_cols]
        return rcopy(res, place, sF, rF.at[own_s], chip_dev((chip + r) % 16))

    def own_work():
        arrived(ain.at[pl.ds(0, 15)], rA)

        def add(r, total):
            return total + ain[r - 1].astype(F32)

        total = lax.fori_loop(1, 16, add, gh[own_s, own_rows, own_cols])
        res[...] = total.astype(BF16)
        fout[core, own_s, own_rows, own_cols] = res[...]

        def push(r, carry):
            peer_copy(r).start()
            return carry

        lax.fori_loop(1, 16, push, 0)

    def cross_out(g, h, other, a, ssem, rsem, peer):
        for q, cols in enumerate(Q):
            zsend[a, H[h], cols] = hdot_nt(g[H[h], cols], mats[other, q]).astype(BF16)
        send(zsend.at[a, H[h]], zsend.at[a + 1, H[h]], ssem, rsem, peer)

    def cross_kept(g, out, section, own, saved, partner, bit):
        for q, cols in enumerate(Q):
            field = g[:, cols]
            out[:, cols] = field + hdot_nt(field, mats[own, q])
            gf[section, pl.ds(32 * bit, 32), cols] = fold_cross(hdot_tn(saved[:, cols], field), masks)
            gf[section, pl.ds(32 * (1 - bit), 32), cols] = fold_cross(hdot_tn(partner[:, cols], field), masks)
        reduce_start(section)

    def cross_in(out, h, a, rsem):
        arrived(zsend.at[a + 1, H[h]], rsem)
        out[H[h]] += zsend[a + 1, H[h]].astype(F32)

    def local_back(g, out, section, saved):
        for q, cols in enumerate(Q):
            field = g[:, cols]
            out[:, cols] = field + hdot_nt(field, mats[section, q])
            full = jnp.where(masks[section], hdot_tn(saved[:, cols].astype(F32), field), 0.0)
            if section == 0:
                gf[0, :, cols] = full[:64] + full[64:]
            else:
                gf[1, pl.ds(0, 32), cols] = full[:32] + full[32:64]
                gf[1, pl.ds(32, 32), cols] = full[64:96] + full[96:]
        reduce_start(section)

    for h in range(2):
        for a in range(2):
            @pl.when(jnp.logical_not((yh == a) & diagonal))
            def _():
                arrived(gin.at[a, H[h]], rG.at[a, h])
        ga[H[h]] = gin[0, H[h]].astype(F32) + gin[1, H[h]].astype(F32)
        cross_out(ga, h, OTHER3, 4, sy, ry.at[2 + h], ypair)
    cross_kept(ga, gb, 3, OWN3, z3, p3, yl)
    last_step()
    for h in range(2):
        cross_in(gb, h, 4, ry.at[2 + h])
        cross_out(gb, h, OTHER2, 6, sx, rx.at[2 + h], xpair)
    cross_kept(gb, gc, 2, OWN2, z2, p2, x % 2)
    arrived(R.at[pl.ds(0, 3), :, 0], rS.at[1])
    px_send(True, 0)
    px_send(True, 1, False)
    for h in range(2):
        cross_in(gc, h, 6, rx.at[2 + h])
    reduce_middle(3)
    local_back(gc, gb, 1, z1)
    local_back(gb, ga, 0, tokens)
    grad_tokens_out = local(ga, grad_tokens_hbm, 5)
    grad_tokens_out.start()
    reduce_middle(2)
    reduce_middle(1)
    reduce_middle(0)
    px_send(True, 1, True)
    pl.when(own_s >= 2)(own_work)
    px_send(True, 2)
    pl.when(own_s < 2)(own_work)
    px_own(True)
    for s in (3, 2, 1, 0):
        @pl.when(own_s != s)
        def _():
            arrived(ain.at[pl.ds(0, 4)], rF.at[s])

        @pl.when(own_s == s)
        def _():
            arrived(ain.at[pl.ds(0, 3)], rF.at[s])

        send(fout.at[core, s], fout.at[core, s], sH, rH.at[s], sibling)
        grad_factors[s, pl.ds(32 * core, 32), :] = fout[core, s].astype(F32)
    factors_out = [local(grad_factors.at[s], grad_factors_hbm.at[s], 7 + s) for s in range(4)]
    for s in (3, 2, 1, 0):
        arrived(fout.at[1 - core, s], rH.at[s])
        grad_factors[s, pl.ds(32 - 32 * core, 32), :] = fout[1 - core, s].astype(F32)
        factors_out[s].start()

    for i, nu, nd in ((0, 1, 2), (1, 2, 1)):
        arrived(px_in.at[0, nu], rP.at[0, nu])
        arrived(px_in.at[1, nd], rP.at[1, nd])
        total = pbuf[i] + px_in[0, nu].astype(F32) + px_in[1, nd].astype(F32)
        proj[pl.ds(256 * i, 256), :] = total.astype(BF16)

    proj_out = local(proj, proj_hbm, 6)
    proj_out.start()
    for copy in (grad_tokens_out, proj_out, *factors_out):
        copy.wait()
    all_sent(zsend.at[pl.ds(0, 2)], sx)
    all_sent(zsend.at[pl.ds(0, 2)], sy)
    all_sent(px_out, sc)
    all_sent(w_oth, sw)
    for b in range(2):
        pl.when(jnp.logical_not((yh == b) & diagonal))(lambda: all_sent(rot, sys.at[b]))
        all_sent(up_out, sR.at[b])
        all_sent(up_out, sZ.at[b])
    all_sent(bsib, sS)
    all_sent(bsib, sB)
    all_sent(px_out, sP)
    pl.when(off_diagonal)(lambda: all_sent(rot, sG.at[0]))
    all_sent(rot, sG.at[1])
    all_sent(cin, sC)
    all_sent(ain.at[pl.ds(0, 15)], sA)
    all_sent(ain.at[pl.ds(0, 15)], sF)
    all_sent(fout.at[0], sH)


def per_device(tokens, weight, factors, cotangent):
    V = pltpu.VMEM
    D = pltpu.SemaphoreType.DMA
    shapes = (
        jax.ShapeDtypeStruct((512, 896), BF16),
        jax.ShapeDtypeStruct((128, 768), F32),
        jax.ShapeDtypeStruct((4, 64, 768), F32),
    )
    hbm = pl.BlockSpec(memory_space=pl.ANY)
    return pl.pallas_call(
        main_kernel,
        out_shape=shapes,
        in_specs=[hbm] * 4,
        out_specs=(hbm,) * 3,
        scratch_shapes=[
            V((128, 768), BF16),
            V((4, 64, 768), F32),
            V((512, 896), BF16),
            V((4, 64, 768), F32),
            V((768, 896), BF16),
            V((6, 6, 128, 128), F32),
            *[V((128, 768), F32)] * 8,
            V((4, 64, 768), F32),
            V((4, 32, 768), F32),
            V((4, 32, 768), F32),
            V((4, 32, 768), BF16),
            V((16, 16, 384), BF16),
            V((16, 384), BF16),
            V((2, 4, 32, 768), BF16),
            V((8, 128, 768), BF16),
            V((128, 768), BF16),
            V((8, 2, 2, 128, 768), BF16),
            V((8, 256, 896), BF16),
            V((768, 896), BF16),
            V((8, 2, 128, 768), BF16),
            V((8, 2, 128, 768), BF16),
            V((8, 2, 128, 768), F32),
            *[V((14, 64, 768), BF16)] * 4,
            V((2, 256, 896), F32),
            V((2, 3, 256, 896), BF16),
            V((2, 3, 256, 896), BF16),
            V((2, 128, 768), BF16),
            V((2, 128, 768), BF16),
            D((11,)),
            D, D((4,)), D, D((4,)),
            D, D((6,)), D, D,
            D((2,)), D((2, 2)),
            D((2,)), D((2, 4, 2)),
            D, D((2,)),
            D, D((8, 2)),
            D((2,)), D((2, 14)),
            D, D((2, 3)),
            D((2,)), D((2, 2)),
            D, D((4,)),
            D, D,
            D, D((4,)),
            D, D((4,)),
        ],
        compiler_params=pltpu.CompilerParams(
            collective_id=0, has_side_effects=True, vmem_limit_bytes=56 * 1024 * 1024
        ),
        name="rotate_project",
    )(tokens, factors, weight, cotangent)


def solution(mesh):
    placed = (P("dp", "tensor"), P("tensor", "dp"), P(None, None, "tensor"), P("tensor", "dp"))
    return jax.shard_map(
        per_device,
        mesh=mesh,
        in_specs=placed,
        out_specs=(P("tensor", "dp"), P("dp", "tensor"), P(None, None, "tensor")),
        check_vma=False,
    )
```

```python
import jax
import jax.numpy as jnp
from jax import lax
from jax.experimental import pallas as pl
from jax.experimental.pallas import tpu as pltpu
from jax.sharding import PartitionSpec as P

F32 = jnp.float32
BF16 = jnp.bfloat16
MESH = pl.DeviceIdType.MESH
Q = [pl.ds(128 * q, 128) for q in range(6)]
U = [pl.ds(256 * u, 256) for u in range(3)]
H = [pl.ds(64 * h, 64) for h in range(2)]
PX = [pl.ds(128 * h, 128) for h in range(2)]
M0, M1, OWN2, OTHER2, OWN3, OTHER3 = range(6)
T0, T1, T2, T3, P2, P3 = 0, 1, 3, 5, 7, 8


def dot(a, b, dims=((1,), (0,))):
    return lax.dot_general(a, b, (dims, ((), ())), preferred_element_type=F32)


def split(a):
    high = a.astype(BF16)
    return high, (a - high.astype(F32)).astype(BF16)


def block_masks():
    r = lax.broadcasted_iota(jnp.int32, (128, 128), 0) // 32
    c = lax.broadcasted_iota(jnp.int32, (128, 128), 1) // 32
    return (r // 2 == c // 2, r % 2 == c % 2, r == c)


def fold_cross(full, masks):
    full = jnp.where(masks[2], full, 0.0)
    return full[:32] + full[32:64] + full[64:96] + full[96:]


def main_kernel(
    tokens_hbm, factors_hbm, w_hbm, cot_hbm,
    proj_hbm, grad_tokens_hbm, grad_factors_hbm,
    tokens, factors, proj, grad_factors, w_own, mats, flipped, z1, z2, z3, ga, gb, gc, gf, cin, gh, ghb, ain, res, fout,
    zsend, rot, R, cotG, w_oth, bsib, bsib_in, bown, up_out, up_in, dn_out, dn_in,
    pbuf, px_kept, px_out, px_in, gsend, gin,
    loc_sem, sx, rx, sy, ry, sc, rc, sw, rw, sys, yr, sR, rR, sS, rS, sB, rB, sZ, rZ, sP, rP,
    sG, rG, sC, rC, sA, rA, sF, rF, sH, rH,
):
    dp, tn = lax.axis_index("dp"), lax.axis_index("tensor")
    core, z, yh = dp % 2, dp // 2 % 8, dp // 16
    x, yl = tn % 4, tn // 4
    chip = yh * 8 + z

    def dev(yh=yh, z=z, core=core, yl=yl, x=x):
        return (yh * 16 + z * 2 + core, yl * 4 + x)

    def chip_dev(index):
        return dev(yh=index // 8, z=index % 8)

    xl, xr, xo = (x + 3) % 4, (x + 1) % 4, (x + 2) % 4
    right, left = dev(x=xr), dev(x=xl)
    xpair = dev(x=x + 1 - 2 * (x % 2))
    ypair = dev(yl=1 - yl)
    sibling = dev(core=1 - core)
    above, below = dev(z=(z + 1) % 8), dev(z=(z + 7) % 8)
    diagonal = yh == yl
    off_diagonal = jnp.logical_not(diagonal)

    def rcopy(src, dst, ssem, rsem, to):
        return pltpu.make_async_remote_copy(
            src_ref=src, dst_ref=dst, send_sem=ssem, recv_sem=rsem,
            device_id=to, device_id_type=MESH,
        )

    def send(src, dst, ssem, rsem, to):
        rcopy(src, dst, ssem, rsem, to).start()

    def arrived(dst, rsem):
        rcopy(dst, dst, rsem, rsem, sibling).wait_recv()

    def all_sent(same_bytes, ssem):
        rcopy(same_bytes, same_bytes, ssem, ssem, sibling).wait_send()

    def local(src, dst, n):
        return pltpu.make_async_copy(src, dst, loc_sem.at[n])

    first = [local(tokens_hbm, tokens, 0), local(factors_hbm, factors, 1)]
    for copy in first:
        copy.start()

    barrier = pltpu.get_barrier_semaphore()

    def greet(r, carry):
        pl.semaphore_signal(barrier, inc=1, device_id=chip_dev((chip + r) % 16), device_id_type=MESH)
        return carry

    lax.fori_loop(1, 16, greet, 0)
    for peer in (right, left, ypair, sibling):
        pl.semaphore_signal(barrier, inc=1, device_id=peer, device_id_type=MESH)
    for peer, here in (
        (dev(yh=0, yl=yh), (yh == 0) & diagonal),
        (dev(yh=1, yl=yh), (yh == 1) & diagonal),
        (dev(yh=yl, yl=0), (yl == 0) & diagonal),
        (dev(yh=yl, yl=1), (yl == 1) & diagonal),
    ):
        @pl.when(jnp.logical_not(here))
        def _():
            pl.semaphore_signal(barrier, inc=1, device_id=peer, device_id_type=MESH)

    own_cot = [local(cot_hbm.at[pl.ds(256 * i, 256)], cotG.at[2 * x + i], 2 + i) for i in range(2)]
    own_w = local(w_hbm, w_own, 4)
    own_w.start()
    for copy in own_cot:
        copy.start()
    for copy in first:
        copy.wait()

    masks = block_masks()
    nothing = jnp.zeros((128, 128), BF16)

    def put_matrix(place, q, stacked, mask):
        u, k = q // 2, q % 2
        rows, rest = pl.ds(128 * k, 128), pl.ds(128 * (1 - k), 128)
        for part, value in enumerate(split(jnp.where(mask, stacked, 0.0))):
            mats[part, place, u, rows, rows] = value
            mats[part, place, u, rows, rest] = nothing

    def put_cross(section, bit, own):
        for q, cols in enumerate(Q):
            for part, place in ((bit, own), (1 - bit, own + 1)):
                coeffs = factors[section, pl.ds(32 * part, 32), cols]
                put_matrix(place, q, jnp.concatenate([coeffs] * 4, 0), masks[2])

    def times(parts, place, u, dims=((1,), (0,))):
        high, low = mats[0, place, u], mats[1, place, u]
        total = dot(parts[0], high, dims) + dot(parts[0], low, dims)
        return total + dot(parts[1], high, dims) if len(parts) > 1 else total

    def times_back(parts, place, u):
        return times(parts, place, u, ((1,), (1,)))

    for q, cols in enumerate(Q):
        c0, c1 = factors[0, :, cols], factors[1, :, cols]
        put_matrix(M0, q, jnp.concatenate([c0, c0], 0), masks[0])
        put_matrix(M1, q, jnp.concatenate([c1[:32], c1[:32], c1[32:], c1[32:]], 0), masks[1])
    for u, cols in enumerate(U):
        field = tokens[:, cols]
        field = field.astype(F32) + times([field], M0, u)
        z1[:, cols] = field
        field = field + times(split(field), M1, u)
        z2[:, cols] = field
        zsend[0, :, cols] = field.astype(BF16)

    pl.semaphore_wait(barrier, 23 - 2 * diagonal.astype(jnp.int32))

    def send_w(i):
        rows = pl.ds(128 * i, 128)
        send(w_hbm.at[rows], w_oth.at[rows], sw, rw, ypair)

    for h in range(2):
        send(zsend.at[0, H[h]], zsend.at[2, H[h]], sx, rx.at[h], xpair)
    for i, to in ((0, right), (1, left), (1, right), (0, left)):
        n = i + (0 if to is right else 2)
        send(cot_hbm.at[pl.ds(256 * i, 256)], cotG.at[2 * x + i], sc, rc.at[n], to)
    send_w(0)
    put_cross(2, x % 2, OWN2)
    put_cross(3, yl, OWN3)
    for u, cols in enumerate(U):
        field = z2[:, cols]
        z3[:, cols] = field + times(split(field), OWN2, u)
    for h in range(2):
        arrived(zsend.at[2, H[h]], rx.at[h])
        for u, cols in enumerate(U):
            field = z3[H[h], cols] + times([zsend[2, H[h], cols]], OTHER2, u)
            z3[H[h], cols] = field
            zsend[1, H[h], cols] = field.astype(BF16)
        send(zsend.at[1, H[h]], zsend.at[3, H[h]], sy, ry.at[h], ypair)

    slot = (yl + yh) % 2

    def to_holder(b, h):
        src = rot.at[H[h]]
        dst = R.at[z, slot, core, H[h]]
        return rcopy(src, dst, sys.at[b], yr.at[slot, h], dev(yh=b, yl=yh))

    for u, cols in enumerate(U):
        field = z3[:, cols]
        gc[:, cols] = field + times(split(field), OWN3, u)
    for h in range(2):
        arrived(zsend.at[3, H[h]], ry.at[h])
        for u, cols in enumerate(U):
            rot[H[h], cols] = (gc[H[h], cols] + times([zsend[3, H[h], cols]], OTHER3, u)).astype(BF16)
        for b in range(2):
            pl.when(jnp.logical_not((yh == b) & diagonal))(to_holder(b, h).start)

    @pl.when(diagonal)
    def _():
        R[z, 0, core] = rot[...]

    def spread(zz, s, up, down, k):
        block = R.at[zz, s, core]
        if up:
            send(block, block, sR.at[0], rR.at[0, k, s], above)
        if down:
            send(block, block, sR.at[1], rR.at[1, k, s], below)
        send(block, block, sS, rS.at[int(k > 2)], sibling)

    @pl.when(off_diagonal)
    def _():
        for h in range(2):
            arrived(R.at[z, 0, core, H[h]], yr.at[0, h])
    spread(z, 0, True, True, 0)
    for h in range(2):
        arrived(R.at[z, 1, core, H[h]], yr.at[1, h])
    spread(z, 1, True, True, 0)
    for i in range(1, 6):
        send_w(i)

    arrived(cotG.at[2 * xl], rc.at[0])
    send(cotG.at[2 * xl], cotG.at[2 * xl], sc, rc.at[4], right)
    arrived(cotG.at[2 * xr + 1], rc.at[3])
    send(cotG.at[2 * xr + 1], cotG.at[2 * xr + 1], sc, rc.at[5], left)

    def step(k, onward):
        lo, hi = (z + 8 - k) % 8, (z + k) % 8
        for s in range(2):
            arrived(R.at[lo, s, core], rR.at[0, k - 1, s])
            spread(lo, s, onward or s == 0, False, k)
            arrived(R.at[hi, s, core], rR.at[1, k - 1, s])
            spread(hi, s, False, onward or s == 0, k)

    def sib_copy(zz, s):
        return rcopy(bsib.at[zz, s], bsib_in.at[zz, s], sB, rB.at[zz, s], sibling)

    def back_unit(xb, s):
        rows = cotG[pl.ds(2 * xb, 2)].reshape(512, 896)
        w = w_oth if s else w_own
        part = lax.dot_general(rows, w[...], (((1,), (1,)), ((), ())), preferred_element_type=F32)
        for c in range(2):
            @pl.when(core == c)
            def _():
                for i in range(2):
                    first, second = 256 * i + 128 * c, 256 * i + 128 * (1 - c)
                    bown[2 * xb + i, s] = part[first:first + 128]
                    bsib[2 * xb + i, s] = part[second:second + 128].astype(BF16)
        for i in range(2):
            sib_copy(2 * xb + i, s).start()

    for copy in own_cot:
        copy.wait()
    own_w.wait()
    back_unit(x, 0)
    for saved, place in ((z1, T1), (z2, T2), (z3, T3)):
        for cols in Q:
            high, low = split(saved[:, cols].T)
            flipped[place, cols] = high
            flipped[place + 1, cols] = low
    step(1, True)
    for cols in Q:
        flipped[T0, cols] = tokens[:, cols].astype(F32).T.astype(BF16)
        flipped[P2, cols] = zsend[2, :, cols].astype(F32).T.astype(BF16)
        flipped[P3, cols] = zsend[3, :, cols].astype(F32).T.astype(BF16)
    arrived(cotG.at[2 * xl + 1], rc.at[1])
    back_unit(xl, 0)
    arrived(cotG.at[2 * xr], rc.at[2])
    back_unit(xr, 0)
    step(2, False)
    arrived(cotG.at[2 * xo], rc.at[4])
    arrived(cotG.at[2 * xo + 1], rc.at[5])
    back_unit(xo, 0)

    def z_at(k):
        return (z + 8 + k) % 8

    def back_ready(s, *places):
        for k in places:
            arrived(bsib_in.at[z_at(k), s], rB.at[z_at(k), s])

    def own_back(zz, s, rows):
        return bown[zz, s, rows] + bsib_in[zz, s, rows].astype(F32)

    def ring_send(s, n):
        for direction in range(2):
            out, into = (dn_out, dn_in) if direction else (up_out, up_in)
            distance = 4 - (n + 1) // 2
            h = direction if n % 2 == 0 else 1 - direction
            value = own_back(z_at(-distance if direction else distance), s, H[h])
            if n >= 2:
                arrived(into.at[7 * s + n - 2], rZ.at[direction, 7 * s + n - 2])
                value = value + into[7 * s + n - 2].astype(F32)
            m = 7 * s + n
            out[m] = value.astype(BF16)
            send(out.at[m], into.at[m], sZ.at[direction], rZ.at[direction, m], below if direction else above)

    def to_owner(s, h):
        return rcopy(gsend.at[s, H[h]], gin.at[yh, H[h]], sG.at[s], rG.at[yh, h], dev(yh=yl, yl=(yl + s) % 2))

    def ring_end(s):
        for h in (1, 0):
            nu, nd = 7 * s + 6 - h, 7 * s + 5 + h
            arrived(up_in.at[nu], rZ.at[0, nu])
            arrived(dn_in.at[nd], rZ.at[1, nd])
            total = own_back(z, s, H[h]) + up_in[nu].astype(F32) + dn_in[nd].astype(F32)
            gsend[s, H[h]] = total.astype(BF16)
            if s == 1:
                to_owner(s, h).start()
            else:
                pl.when(off_diagonal)(to_owner(s, h).start)

                @pl.when(diagonal)
                def _():
                    gin[yh, H[h]] = gsend[0, H[h]]

    def product(zz):
        return jnp.dot(R[zz, 0].reshape(256, 768), w_own[...], preferred_element_type=F32) + jnp.dot(
            R[zz, 1].reshape(256, 768), w_oth[...], preferred_element_type=F32
        )

    def in_phase(zz, late):
        away = (zz - z + 8) % 8
        return ((away >= 3) & (away <= 5)) == late

    def px_place(direction, n):
        return ((2 * xo + 1, 2 * xr, 2 * xr + 1), (2 * xo, 2 * xl + 1, 2 * xl))[direction][n]

    def px_arrived(direction, n, h):
        arrived(px_in.at[direction, n, PX[h]], rP.at[direction, 2 * n + h])

    def px_post(direction, n, h, part):
        if n == 2:
            px_arrived(direction, 0, h)
            part = part + px_in[direction, 0, PX[h]].astype(F32)
        px_out[direction, n, PX[h]] = part.astype(BF16)
        send(
            px_out.at[direction, n, PX[h]], px_in.at[direction, n, PX[h]], sP,
            rP.at[direction, 2 * n + h], left if direction else right,
        )

    def px_send(late, n, after_far=None):
        for direction in range(2):
            now = in_phase(px_place(direction, n), late)
            if after_far is not None:
                now = now & in_phase(px_place(direction, 0), after_far)

            @pl.when(now)
            def _():
                value = product(px_place(direction, n))
                for h in range(2):
                    px_post(direction, n, h, value[128 * h:128 * h + 128])

    def px_last(h):
        for direction in range(2):
            @pl.when(in_phase(px_place(direction, 2), True))
            def _():
                if h == 0:
                    value = product(px_place(direction, 2))
                    px_post(direction, 2, 0, value[:128])
                    px_kept[direction] = value[128:]
                else:
                    px_post(direction, 2, 1, px_kept[direction])

    def px_own(late):
        for i in range(2):
            @pl.when(in_phase(2 * x + i, late))
            def _():
                pbuf[i] = product(2 * x + i)

    def third_step(s):
        lo, hi = z_at(-3), z_at(3)
        arrived(R.at[lo, s, core], rR.at[0, 2, s])
        spread(lo, s, False, False, 3)
        arrived(R.at[hi, s, core], rR.at[1, 2, s])
        spread(hi, s, False, s == 1, 3)

    def last_step():
        zf = z_at(4)
        for s in range(2):
            arrived(R.at[zf, s, core], rR.at[s, 3, s])
            spread(zf, s, False, False, 4)

    back_ready(0, 4, 3, -3)
    ring_send(0, 0)
    ring_send(0, 1)
    back_ready(0, 2, -2, 1, -1, 0)
    ring_send(0, 2)
    ring_send(0, 3)
    arrived(w_oth, rw)
    far = z_at(4) // 2
    turn = 2 * (z % 2) - 1
    back_unit(far, 1)
    ring_send(0, 4)
    arrived(R.at[pl.ds(0, 5), :, 0], rS.at[0])
    px_send(False, 0)
    ring_send(0, 5)
    back_unit((far + 4 + turn) % 4, 1)
    ring_send(0, 6)
    back_ready(1, 4, 3, -3)
    ring_send(1, 0)
    ring_send(1, 1)
    back_unit((far + 4 - turn) % 4, 1)
    third_step(0)
    back_unit((far + 2) % 4, 1)
    px_send(False, 1)
    ring_send(1, 2)
    ring_end(0)
    back_ready(1, 2, -2)
    ring_send(1, 3)
    px_send(False, 2)
    ring_send(1, 4)
    back_ready(1, 1, -1, 0)
    ring_send(1, 5)
    px_own(False)
    ring_send(1, 6)
    ring_end(1)
    held = ((z_at(-2), 1, 0, 2, above), (z_at(2), 1, 1, 2, below), (z_at(-3), 0, 0, 3, above))
    for zz, s, direction, k, to in held:
        block = R.at[zz, s, core]
        send(block, block, sR.at[direction], rR.at[direction, k, s], to)
    third_step(1)

    def reduce_start(s):
        send(gf.at[s, pl.ds(32 * (1 - core), 32)], cin.at[s], sC, rC.at[s], sibling)

    def piece(j):
        return (pl.ds(16 * (j // 2), 16), pl.ds(384 * (j % 2), 384))

    def owner_of(s, j):
        return 8 * (j % 2) + 4 * (j // 2) + s

    def owner_copy(s, j):
        owner = owner_of(s, j)
        r = (chip + 16 - owner) % 16
        src = ghb.at[s, piece(j)[0], piece(j)[1]]
        return r, rcopy(src, ain.at[(r + 15) % 16], sA, rA, chip_dev(owner))

    def reduce_middle(s):
        arrived(cin.at[s], rC.at[s])
        gh[s] = gf[s, pl.ds(32 * core, 32), :] + cin[s]
        ghb[s] = gh[s].astype(BF16)
        for j in range(4):
            r, copy = owner_copy(s, j)
            pl.when(r != 0)(copy.start)

    own_s = z % 4
    own_rows, own_cols = pl.ds(16 * (z // 4), 16), pl.ds(384 * yh, 384)

    def peer_copy(r):
        place = fout.at[core, own_s, own_rows, own_cols]
        return rcopy(res, place, sF, rF.at[own_s], chip_dev((chip + r) % 16))

    def own_work():
        arrived(ain.at[pl.ds(0, 15)], rA)

        def add(r, total):
            return total + ain[r - 1].astype(F32)

        total = lax.fori_loop(1, 16, add, gh[own_s, own_rows, own_cols])
        res[...] = total.astype(BF16)
        fout[core, own_s, own_rows, own_cols] = res[...]

        for r in (4, 12, 3, 5, 11, 13, 2, 6, 10, 14, 1, 7, 9, 15, 8):
            peer_copy(r).start()

    def cross_out(g, h, other, a, ssem, rsem, peer):
        for u, cols in enumerate(U):
            zsend[a, H[h], cols] = times_back(split(g[H[h], cols]), other, u).astype(BF16)
        send(zsend.at[a, H[h]], zsend.at[a + 1, H[h]], ssem, rsem, peer)

    def products_with(parts, place, u, exact):
        total = dot(flipped[place, U[u]], parts[0]) + dot(flipped[place, U[u]], parts[1])
        return total if exact else total + dot(flipped[place + 1, U[u]], parts[0])

    def diagonals(full, u):
        return ((full[:128, :128], Q[2 * u]), (full[128:, 128:], Q[2 * u + 1]))

    def cross_kept(g, out, section, own, saved, partner, bit):
        for u, cols in enumerate(U):
            field = g[:, cols]
            parts = split(field)
            out[:, cols] = field + times_back(parts, own, u)
            for place, exact, side in ((saved, False, bit), (partner, True, 1 - bit)):
                for full, q in diagonals(products_with(parts, place, u, exact), u):
                    gf[section, pl.ds(32 * side, 32), q] = fold_cross(full, masks)
        reduce_start(section)

    def cross_in(out, h, a, rsem):
        arrived(zsend.at[a + 1, H[h]], rsem)
        out[H[h]] += zsend[a + 1, H[h]].astype(F32)

    def local_back(g, out, section, saved):
        for u, cols in enumerate(U):
            field = g[:, cols]
            parts = split(field)
            out[:, cols] = field + times_back(parts, section, u)
            for full, q in diagonals(products_with(parts, saved, u, section == 0), u):
                full = jnp.where(masks[section], full, 0.0)
                if section == 0:
                    gf[0, :, q] = full[:64] + full[64:]
                else:
                    gf[1, pl.ds(0, 32), q] = full[:32] + full[32:64]
                    gf[1, pl.ds(32, 32), q] = full[64:96] + full[96:]
        reduce_start(section)

    for h in range(2):
        for a in range(2):
            @pl.when(jnp.logical_not((yh == a) & diagonal))
            def _():
                arrived(gin.at[a, H[h]], rG.at[a, h])
        ga[H[h]] = gin[0, H[h]].astype(F32) + gin[1, H[h]].astype(F32)
        cross_out(ga, h, OTHER3, 4, sy, ry.at[2 + h], ypair)
    cross_kept(ga, gb, 3, OWN3, T3, P3, yl)
    last_step()
    for h in range(2):
        cross_in(gb, h, 4, ry.at[2 + h])
        cross_out(gb, h, OTHER2, 6, sx, rx.at[2 + h], xpair)
    cross_kept(gb, gc, 2, OWN2, T2, P2, x % 2)
    arrived(R.at[pl.ds(0, 3), :, 0], rS.at[1])
    px_send(True, 0)
    px_send(True, 1, False)
    for h in range(2):
        cross_in(gc, h, 6, rx.at[2 + h])
    reduce_middle(3)
    local_back(gc, gb, 1, T1)
    local_back(gb, ga, 0, T0)
    grad_tokens_out = local(ga, grad_tokens_hbm, 5)
    grad_tokens_out.start()
    reduce_middle(2)
    reduce_middle(1)
    reduce_middle(0)
    px_last(0)
    px_send(True, 1, True)
    pl.when(own_s >= 2)(own_work)
    pl.when(own_s < 2)(own_work)
    px_last(1)
    px_own(True)
    for s in (3, 2, 1, 0):
        @pl.when(own_s != s)
        def _():
            arrived(ain.at[pl.ds(0, 4)], rF.at[s])

        @pl.when(own_s == s)
        def _():
            arrived(ain.at[pl.ds(0, 3)], rF.at[s])

        send(fout.at[core, s], fout.at[core, s], sH, rH.at[s], sibling)
        grad_factors[s, pl.ds(32 * core, 32), :] = fout[core, s].astype(F32)
    factors_out = [local(grad_factors.at[s], grad_factors_hbm.at[s], 7 + s) for s in range(4)]
    for s in (3, 2, 1, 0):
        arrived(fout.at[1 - core, s], rH.at[s])
        grad_factors[s, pl.ds(32 - 32 * core, 32), :] = fout[1 - core, s].astype(F32)
        factors_out[s].start()

    for i, nu, nd in ((0, 1, 2), (1, 2, 1)):
        for h in range(2):
            px_arrived(0, nu, h)
            px_arrived(1, nd, h)
        total = pbuf[i] + px_in[0, nu].astype(F32) + px_in[1, nd].astype(F32)
        proj[pl.ds(256 * i, 256), :] = total.astype(BF16)

    proj_out = local(proj, proj_hbm, 6)
    proj_out.start()
    for copy in (grad_tokens_out, proj_out, *factors_out):
        copy.wait()
    all_sent(zsend.at[pl.ds(0, 2)], sx)
    all_sent(zsend.at[pl.ds(0, 2)], sy)
    all_sent(px_out, sc)
    all_sent(w_oth, sw)
    for b in range(2):
        pl.when(jnp.logical_not((yh == b) & diagonal))(lambda: all_sent(rot, sys.at[b]))
        all_sent(up_out, sR.at[b])
        all_sent(up_out, sZ.at[b])
    all_sent(bsib, sS)
    all_sent(bsib, sB)
    all_sent(px_out, sP)
    pl.when(off_diagonal)(lambda: all_sent(rot, sG.at[0]))
    all_sent(rot, sG.at[1])
    all_sent(cin, sC)
    all_sent(ain.at[pl.ds(0, 15)], sA)
    all_sent(ain.at[pl.ds(0, 15)], sF)
    all_sent(fout.at[0], sH)


def per_device(tokens, weight, factors, cotangent):
    V = pltpu.VMEM
    D = pltpu.SemaphoreType.DMA
    shapes = (
        jax.ShapeDtypeStruct((512, 896), BF16),
        jax.ShapeDtypeStruct((128, 768), F32),
        jax.ShapeDtypeStruct((4, 64, 768), F32),
    )
    hbm = pl.BlockSpec(memory_space=pl.ANY)
    return pl.pallas_call(
        main_kernel,
        out_shape=shapes,
        in_specs=[hbm] * 4,
        out_specs=(hbm,) * 3,
        scratch_shapes=[
            V((128, 768), BF16),
            V((4, 64, 768), F32),
            V((512, 896), BF16),
            V((4, 64, 768), F32),
            V((768, 896), BF16),
            V((2, 6, 3, 256, 256), BF16),
            V((9, 768, 128), BF16),
            *[V((128, 768), F32)] * 6,
            V((4, 64, 768), F32),
            V((4, 32, 768), F32),
            V((4, 32, 768), F32),
            V((4, 32, 768), BF16),
            V((16, 16, 384), BF16),
            V((16, 384), BF16),
            V((2, 4, 32, 768), BF16),
            V((8, 128, 768), BF16),
            V((128, 768), BF16),
            V((8, 2, 2, 128, 768), BF16),
            V((8, 256, 896), BF16),
            V((768, 896), BF16),
            V((8, 2, 128, 768), BF16),
            V((8, 2, 128, 768), BF16),
            V((8, 2, 128, 768), F32),
            *[V((14, 64, 768), BF16)] * 4,
            V((2, 256, 896), F32),
            V((2, 128, 896), F32),
            V((2, 3, 256, 896), BF16),
            V((2, 3, 256, 896), BF16),
            V((2, 128, 768), BF16),
            V((2, 128, 768), BF16),
            D((11,)),
            D, D((4,)), D, D((4,)),
            D, D((6,)), D, D,
            D((2,)), D((2, 2)),
            D((2,)), D((2, 4, 2)),
            D, D((2,)),
            D, D((8, 2)),
            D((2,)), D((2, 14)),
            D, D((2, 6)),
            D((2,)), D((2, 2)),
            D, D((4,)),
            D, D,
            D, D((4,)),
            D, D((4,)),
        ],
        compiler_params=pltpu.CompilerParams(
            collective_id=0, has_side_effects=True, vmem_limit_bytes=60 * 1024 * 1024
        ),
        name="rotate_project",
    )(tokens, factors, weight, cotangent)


def solution(mesh):
    placed = (P("dp", "tensor"), P("tensor", "dp"), P(None, None, "tensor"), P("tensor", "dp"))
    return jax.shard_map(
        per_device,
        mesh=mesh,
        in_specs=placed,
        out_specs=(P("tensor", "dp"), P("dp", "tensor"), P(None, None, "tensor")),
        check_vma=False,
    )
```

```python
import jax
import jax.numpy as jnp
from jax import lax
from jax.experimental import pallas as pl
from jax.experimental.pallas import tpu as pltpu
from jax.sharding import PartitionSpec as P

F32 = jnp.float32
BF16 = jnp.bfloat16
MESH = pl.DeviceIdType.MESH
Q = [pl.ds(128 * q, 128) for q in range(6)]
U = [pl.ds(256 * u, 256) for u in range(3)]
H = [pl.ds(64 * h, 64) for h in range(2)]
PX = [pl.ds(128 * h, 128) for h in range(2)]
M0, M1, OWN2, OTHER2, OWN3, OTHER3 = range(6)
T0, T1, T2, T3, P2, P3 = 0, 1, 3, 5, 7, 8


def dot(a, b, dims=((1,), (0,))):
    return lax.dot_general(a, b, (dims, ((), ())), preferred_element_type=F32)


def split(a):
    high = a.astype(BF16)
    return high, (a - high.astype(F32)).astype(BF16)


def block_masks():
    r = lax.broadcasted_iota(jnp.int32, (128, 128), 0) // 32
    c = lax.broadcasted_iota(jnp.int32, (128, 128), 1) // 32
    return (r // 2 == c // 2, r % 2 == c % 2, r == c)


def fold_cross(full, masks):
    full = jnp.where(masks[2], full, 0.0)
    return full[:32] + full[32:64] + full[64:96] + full[96:]


def main_kernel(
    tokens_hbm, factors_hbm, w_hbm, cot_hbm,
    proj_hbm, grad_tokens_hbm, grad_factors_hbm,
    tokens, factors, proj, grad_factors, w_own, mats, flipped, z1, z2, z3, ga, gb, gc, gf, cin, gh, ghb, ain, res, fout,
    zsend, rot, R, cotG, w_oth, bsib, bsib_in, bown, up_out, up_in, dn_out, dn_in,
    pbuf, px_kept, px_out, px_in, gsend, gin,
    loc_sem, sx, rx, sy, ry, sc, rc, sw, rw, sys, yr, sR, rR, sS, rS, sB, rB, sZ, rZ, sP, rP,
    sG, rG, sC, rC, sA, rA, sF, rF, sH, rH,
):
    dp, tn = lax.axis_index("dp"), lax.axis_index("tensor")
    core, z, yh = dp % 2, dp // 2 % 8, dp // 16
    x, yl = tn % 4, tn // 4
    chip = yh * 8 + z

    def dev(yh=yh, z=z, core=core, yl=yl, x=x):
        return (yh * 16 + z * 2 + core, yl * 4 + x)

    def chip_dev(index):
        return dev(yh=index // 8, z=index % 8)

    xl, xr, xo = (x + 3) % 4, (x + 1) % 4, (x + 2) % 4
    right, left = dev(x=xr), dev(x=xl)
    xpair = dev(x=x + 1 - 2 * (x % 2))
    ypair = dev(yl=1 - yl)
    sibling = dev(core=1 - core)
    above, below = dev(z=(z + 1) % 8), dev(z=(z + 7) % 8)
    diagonal = yh == yl
    off_diagonal = jnp.logical_not(diagonal)

    def rcopy(src, dst, ssem, rsem, to):
        return pltpu.make_async_remote_copy(
            src_ref=src, dst_ref=dst, send_sem=ssem, recv_sem=rsem,
            device_id=to, device_id_type=MESH,
        )

    def send(src, dst, ssem, rsem, to):
        rcopy(src, dst, ssem, rsem, to).start()

    def arrived(dst, rsem):
        rcopy(dst, dst, rsem, rsem, sibling).wait_recv()

    def all_sent(same_bytes, ssem):
        rcopy(same_bytes, same_bytes, ssem, ssem, sibling).wait_send()

    def local(src, dst, n):
        return pltpu.make_async_copy(src, dst, loc_sem.at[n])

    first = [local(tokens_hbm, tokens, 0), local(factors_hbm, factors, 1)]
    for copy in first:
        copy.start()

    barrier = pltpu.get_barrier_semaphore()

    def greet(r, carry):
        pl.semaphore_signal(barrier, inc=1, device_id=chip_dev((chip + r) % 16), device_id_type=MESH)
        return carry

    lax.fori_loop(1, 16, greet, 0)
    for peer in (right, left, ypair, sibling):
        pl.semaphore_signal(barrier, inc=1, device_id=peer, device_id_type=MESH)
    for peer, here in (
        (dev(yh=0, yl=yh), (yh == 0) & diagonal),
        (dev(yh=1, yl=yh), (yh == 1) & diagonal),
        (dev(yh=yl, yl=0), (yl == 0) & diagonal),
        (dev(yh=yl, yl=1), (yl == 1) & diagonal),
    ):
        @pl.when(jnp.logical_not(here))
        def _():
            pl.semaphore_signal(barrier, inc=1, device_id=peer, device_id_type=MESH)

    own_cot = [local(cot_hbm.at[pl.ds(256 * i, 256)], cotG.at[2 * x + i], 2 + i) for i in range(2)]
    own_w = local(w_hbm, w_own, 4)
    own_w.start()
    for copy in own_cot:
        copy.start()
    for copy in first:
        copy.wait()

    masks = block_masks()
    nothing = jnp.zeros((128, 128), BF16)

    def put_matrix(place, q, stacked, mask):
        u, k = q // 2, q % 2
        rows, rest = pl.ds(128 * k, 128), pl.ds(128 * (1 - k), 128)
        for part, value in enumerate(split(jnp.where(mask, stacked, 0.0))):
            mats[part, place, u, rows, rows] = value
            mats[part, place, u, rows, rest] = nothing

    def put_cross(section, bit, own):
        for q, cols in enumerate(Q):
            for part, place in ((bit, own), (1 - bit, own + 1)):
                coeffs = factors[section, pl.ds(32 * part, 32), cols]
                put_matrix(place, q, jnp.concatenate([coeffs] * 4, 0), masks[2])

    def times(parts, place, u, dims=((1,), (0,))):
        high, low = mats[0, place, u], mats[1, place, u]
        total = dot(parts[0], high, dims) + dot(parts[0], low, dims)
        return total + dot(parts[1], high, dims) if len(parts) > 1 else total

    def times_back(parts, place, u):
        return times(parts, place, u, ((1,), (1,)))

    for q, cols in enumerate(Q):
        c0, c1 = factors[0, :, cols], factors[1, :, cols]
        put_matrix(M0, q, jnp.concatenate([c0, c0], 0), masks[0])
        put_matrix(M1, q, jnp.concatenate([c1[:32], c1[:32], c1[32:], c1[32:]], 0), masks[1])
    for u, cols in enumerate(U):
        field = tokens[:, cols]
        field = field.astype(F32) + times([field], M0, u)
        z1[:, cols] = field
        field = field + times(split(field), M1, u)
        z2[:, cols] = field
        zsend[0, :, cols] = field.astype(BF16)

    pl.semaphore_wait(barrier, 23 - 2 * diagonal.astype(jnp.int32))

    def send_w(i):
        rows = pl.ds(128 * i, 128)
        send(w_hbm.at[rows], w_oth.at[rows], sw, rw, ypair)

    for h in range(2):
        send(zsend.at[0, H[h]], zsend.at[2, H[h]], sx, rx.at[h], xpair)
    for i, to in ((0, right), (1, left), (1, right), (0, left)):
        n = i + (0 if to is right else 2)
        send(cot_hbm.at[pl.ds(256 * i, 256)], cotG.at[2 * x + i], sc, rc.at[n], to)
    send_w(0)
    put_cross(2, x % 2, OWN2)
    put_cross(3, yl, OWN3)
    for u, cols in enumerate(U):
        field = z2[:, cols]
        z3[:, cols] = field + times(split(field), OWN2, u)
    for h in range(2):
        arrived(zsend.at[2, H[h]], rx.at[h])
        for u, cols in enumerate(U):
            field = z3[H[h], cols] + times([zsend[2, H[h], cols]], OTHER2, u)
            z3[H[h], cols] = field
            zsend[1, H[h], cols] = field.astype(BF16)
        send(zsend.at[1, H[h]], zsend.at[3, H[h]], sy, ry.at[h], ypair)

    slot = (yl + yh) % 2

    def to_holder(b, h):
        src = rot.at[H[h]]
        dst = R.at[z, slot, core, H[h]]
        return rcopy(src, dst, sys.at[b], yr.at[slot, h], dev(yh=b, yl=yh))

    for u, cols in enumerate(U):
        field = z3[:, cols]
        gc[:, cols] = field + times(split(field), OWN3, u)
    for h in range(2):
        arrived(zsend.at[3, H[h]], ry.at[h])
        for u, cols in enumerate(U):
            rot[H[h], cols] = (gc[H[h], cols] + times([zsend[3, H[h], cols]], OTHER3, u)).astype(BF16)
        for b in range(2):
            pl.when(jnp.logical_not((yh == b) & diagonal))(to_holder(b, h).start)

    @pl.when(diagonal)
    def _():
        R[z, 0, core] = rot[...]

    def spread(zz, s, up, down, k):
        block = R.at[zz, s, core]
        if up:
            send(block, block, sR.at[0], rR.at[0, k, s], above)
        if down:
            send(block, block, sR.at[1], rR.at[1, k, s], below)
        send(block, block, sS, rS.at[int(k > 2)], sibling)

    @pl.when(off_diagonal)
    def _():
        for h in range(2):
            arrived(R.at[z, 0, core, H[h]], yr.at[0, h])
    spread(z, 0, True, True, 0)
    for h in range(2):
        arrived(R.at[z, 1, core, H[h]], yr.at[1, h])
    spread(z, 1, True, True, 0)
    for i in range(1, 6):
        send_w(i)

    arrived(cotG.at[2 * xl], rc.at[0])
    send(cotG.at[2 * xl], cotG.at[2 * xl], sc, rc.at[4], right)
    arrived(cotG.at[2 * xr + 1], rc.at[3])
    send(cotG.at[2 * xr + 1], cotG.at[2 * xr + 1], sc, rc.at[5], left)

    def step(k, onward):
        lo, hi = (z + 8 - k) % 8, (z + k) % 8
        for s in range(2):
            arrived(R.at[lo, s, core], rR.at[0, k - 1, s])
            spread(lo, s, onward or s == 0, False, k)
            arrived(R.at[hi, s, core], rR.at[1, k - 1, s])
            spread(hi, s, False, onward or s == 0, k)

    def sib_copy(zz, s):
        return rcopy(bsib.at[zz, s], bsib_in.at[zz, s], sB, rB.at[zz, s], sibling)

    def back_unit(xb, s):
        rows = cotG[pl.ds(2 * xb, 2)].reshape(512, 896)
        w = w_oth if s else w_own
        part = lax.dot_general(rows, w[...], (((1,), (1,)), ((), ())), preferred_element_type=F32)
        for c in range(2):
            @pl.when(core == c)
            def _():
                for i in range(2):
                    first, second = 256 * i + 128 * c, 256 * i + 128 * (1 - c)
                    bown[2 * xb + i, s] = part[first:first + 128]
                    bsib[2 * xb + i, s] = part[second:second + 128].astype(BF16)
        for i in range(2):
            sib_copy(2 * xb + i, s).start()

    for copy in own_cot:
        copy.wait()
    own_w.wait()
    back_unit(x, 0)
    for saved, place in ((z1, T1), (z2, T2), (z3, T3)):
        for cols in Q:
            high, low = split(saved[:, cols].T)
            flipped[place, cols] = high
            flipped[place + 1, cols] = low
    step(1, True)
    for cols in Q:
        flipped[T0, cols] = tokens[:, cols].astype(F32).T.astype(BF16)
        flipped[P2, cols] = zsend[2, :, cols].astype(F32).T.astype(BF16)
        flipped[P3, cols] = zsend[3, :, cols].astype(F32).T.astype(BF16)
    arrived(cotG.at[2 * xl + 1], rc.at[1])
    back_unit(xl, 0)
    arrived(cotG.at[2 * xr], rc.at[2])
    back_unit(xr, 0)
    step(2, False)
    arrived(cotG.at[2 * xo], rc.at[4])
    arrived(cotG.at[2 * xo + 1], rc.at[5])
    back_unit(xo, 0)

    def z_at(k):
        return (z + 8 + k) % 8

    def back_ready(s, *places):
        for k in places:
            arrived(bsib_in.at[z_at(k), s], rB.at[z_at(k), s])

    def own_back(zz, s, rows):
        return bown[zz, s, rows] + bsib_in[zz, s, rows].astype(F32)

    def ring_send(s, n):
        for direction in range(2):
            out, into = (dn_out, dn_in) if direction else (up_out, up_in)
            distance = 4 - (n + 1) // 2
            h = direction if n % 2 == 0 else 1 - direction
            value = own_back(z_at(-distance if direction else distance), s, H[h])
            if n >= 2:
                arrived(into.at[7 * s + n - 2], rZ.at[direction, 7 * s + n - 2])
                value = value + into[7 * s + n - 2].astype(F32)
            m = 7 * s + n
            out[m] = value.astype(BF16)
            send(out.at[m], into.at[m], sZ.at[direction], rZ.at[direction, m], below if direction else above)

    def to_owner(s, h):
        return rcopy(gsend.at[s, H[h]], gin.at[yh, H[h]], sG.at[s], rG.at[yh, h], dev(yh=yl, yl=(yl + s) % 2))

    def ring_end(s):
        for h in (1, 0):
            nu, nd = 7 * s + 6 - h, 7 * s + 5 + h
            arrived(up_in.at[nu], rZ.at[0, nu])
            arrived(dn_in.at[nd], rZ.at[1, nd])
            total = own_back(z, s, H[h]) + up_in[nu].astype(F32) + dn_in[nd].astype(F32)
            gsend[s, H[h]] = total.astype(BF16)
            if s == 1:
                to_owner(s, h).start()
            else:
                pl.when(off_diagonal)(to_owner(s, h).start)

                @pl.when(diagonal)
                def _():
                    gin[yh, H[h]] = gsend[0, H[h]]

    def product(zz):
        return jnp.dot(R[zz, 0].reshape(256, 768), w_own[...], preferred_element_type=F32) + jnp.dot(
            R[zz, 1].reshape(256, 768), w_oth[...], preferred_element_type=F32
        )

    def in_phase(zz, late):
        away = (zz - z + 8) % 8
        return ((away >= 3) & (away <= 5)) == late

    def px_place(direction, n):
        return ((2 * xo + 1, 2 * xr, 2 * xr + 1), (2 * xo, 2 * xl + 1, 2 * xl))[direction][n]

    def px_arrived(direction, n, h):
        arrived(px_in.at[direction, n, PX[h]], rP.at[direction, 2 * n + h])

    def px_post(direction, n, h, part):
        if n == 2:
            px_arrived(direction, 0, h)
            part = part + px_in[direction, 0, PX[h]].astype(F32)
        px_out[direction, n, PX[h]] = part.astype(BF16)
        send(
            px_out.at[direction, n, PX[h]], px_in.at[direction, n, PX[h]], sP,
            rP.at[direction, 2 * n + h], left if direction else right,
        )

    def px_send(late, n, after_far=None):
        for direction in range(2):
            now = in_phase(px_place(direction, n), late)
            if after_far is not None:
                now = now & in_phase(px_place(direction, 0), after_far)

            @pl.when(now)
            def _():
                value = product(px_place(direction, n))
                for h in range(2):
                    px_post(direction, n, h, value[128 * h:128 * h + 128])

    def px_last(h):
        for direction in range(2):
            @pl.when(in_phase(px_place(direction, 2), True))
            def _():
                if h == 0:
                    value = product(px_place(direction, 2))
                    px_post(direction, 2, 0, value[:128])
                    px_kept[direction] = value[128:]
                else:
                    px_post(direction, 2, 1, px_kept[direction])

    def px_own(late):
        for i in range(2):
            @pl.when(in_phase(2 * x + i, late))
            def _():
                pbuf[i] = product(2 * x + i)

    def third_step(s):
        lo, hi = z_at(-3), z_at(3)
        arrived(R.at[lo, s, core], rR.at[0, 2, s])
        spread(lo, s, False, False, 3)
        arrived(R.at[hi, s, core], rR.at[1, 2, s])
        spread(hi, s, False, s == 1, 3)

    def last_step():
        zf = z_at(4)
        for s in range(2):
            arrived(R.at[zf, s, core], rR.at[s, 3, s])
            spread(zf, s, False, False, 4)

    back_ready(0, 4, 3, -3)
    ring_send(0, 0)
    ring_send(0, 1)
    back_ready(0, 2, -2, 1, -1, 0)
    ring_send(0, 2)
    ring_send(0, 3)
    arrived(w_oth, rw)
    far = z_at(4) // 2
    turn = 2 * (z % 2) - 1
    back_unit(far, 1)
    ring_send(0, 4)
    arrived(R.at[pl.ds(0, 5), :, 0], rS.at[0])
    px_send(False, 0)
    ring_send(0, 5)
    back_unit((far + 4 + turn) % 4, 1)
    ring_send(0, 6)
    back_ready(1, 4, 3, -3)
    ring_send(1, 0)
    ring_send(1, 1)
    back_unit((far + 4 - turn) % 4, 1)
    third_step(0)
    back_unit((far + 2) % 4, 1)
    px_send(False, 1)
    ring_send(1, 2)
    ring_end(0)
    back_ready(1, 2, -2)
    ring_send(1, 3)
    px_send(False, 2)
    ring_send(1, 4)
    back_ready(1, 1, -1, 0)
    ring_send(1, 5)
    px_own(False)
    ring_send(1, 6)
    ring_end(1)
    held = ((z_at(-2), 1, 0, 2, above), (z_at(2), 1, 1, 2, below), (z_at(-3), 0, 0, 3, above))
    for zz, s, direction, k, to in held:
        block = R.at[zz, s, core]
        send(block, block, sR.at[direction], rR.at[direction, k, s], to)
    third_step(1)

    def reduce_start(s):
        send(gf.at[s, pl.ds(32 * (1 - core), 32)], cin.at[s], sC, rC.at[s], sibling)

    def piece(j):
        return (pl.ds(16 * (j // 2), 16), pl.ds(384 * (j % 2), 384))

    def owner_of(s, j):
        return 8 * (j % 2) + 4 * (j // 2) + s

    def owner_copy(s, j):
        owner = owner_of(s, j)
        r = (chip + 16 - owner) % 16
        src = ghb.at[s, piece(j)[0], piece(j)[1]]
        return r, rcopy(src, ain.at[(r + 15) % 16], sA, rA, chip_dev(owner))

    def reduce_middle(s):
        arrived(cin.at[s], rC.at[s])
        gh[s] = gf[s, pl.ds(32 * core, 32), :] + cin[s]
        ghb[s] = gh[s].astype(BF16)
        for j in range(4):
            r, copy = owner_copy(s, j)
            pl.when(r != 0)(copy.start)

    own_s = z % 4
    own_rows, own_cols = pl.ds(16 * (z // 4), 16), pl.ds(384 * yh, 384)

    def peer_copy(r):
        place = fout.at[core, own_s, own_rows, own_cols]
        return rcopy(res, place, sF, rF.at[own_s], chip_dev((chip + r) % 16))

    def own_work():
        arrived(ain.at[pl.ds(0, 15)], rA)

        def add(r, total):
            return total + ain[r - 1].astype(F32)

        total = lax.fori_loop(1, 16, add, gh[own_s, own_rows, own_cols])
        res[...] = total.astype(BF16)
        fout[core, own_s, own_rows, own_cols] = res[...]

        for r in (4, 12, 3, 5, 11, 13, 2, 6, 10, 14, 1, 7, 9, 15, 8):
            peer_copy(r).start()

    def cross_out(g, h, other, a, ssem, rsem, peer):
        for u, cols in enumerate(U):
            zsend[a, H[h], cols] = times_back(split(g[H[h], cols]), other, u).astype(BF16)
        send(zsend.at[a, H[h]], zsend.at[a + 1, H[h]], ssem, rsem, peer)

    def products_with(parts, place, u, exact):
        total = dot(flipped[place, U[u]], parts[0]) + dot(flipped[place, U[u]], parts[1])
        return total if exact else total + dot(flipped[place + 1, U[u]], parts[0])

    def diagonals(full, u):
        return ((full[:128, :128], Q[2 * u]), (full[128:, 128:], Q[2 * u + 1]))

    def cross_kept(g, out, section, own, saved, partner, bit):
        for u, cols in enumerate(U):
            field = g[:, cols]
            parts = split(field)
            out[:, cols] = field + times_back(parts, own, u)
            for place, exact, side in ((saved, False, bit), (partner, True, 1 - bit)):
                for full, q in diagonals(products_with(parts, place, u, exact), u):
                    gf[section, pl.ds(32 * side, 32), q] = fold_cross(full, masks)
        reduce_start(section)

    def cross_in(out, h, a, rsem):
        arrived(zsend.at[a + 1, H[h]], rsem)
        out[H[h]] += zsend[a + 1, H[h]].astype(F32)

    def local_back(g, out, section, saved):
        for u, cols in enumerate(U):
            field = g[:, cols]
            parts = split(field)
            out[:, cols] = field + times_back(parts, section, u)
            for full, q in diagonals(products_with(parts, saved, u, section == 0), u):
                full = jnp.where(masks[section], full, 0.0)
                if section == 0:
                    gf[0, :, q] = full[:64] + full[64:]
                else:
                    gf[1, pl.ds(0, 32), q] = full[:32] + full[32:64]
                    gf[1, pl.ds(32, 32), q] = full[64:96] + full[96:]
        reduce_start(section)

    for h in range(2):
        for a in range(2):
            @pl.when(jnp.logical_not((yh == a) & diagonal))
            def _():
                arrived(gin.at[a, H[h]], rG.at[a, h])
        ga[H[h]] = gin[0, H[h]].astype(F32) + gin[1, H[h]].astype(F32)
        cross_out(ga, h, OTHER3, 4, sy, ry.at[2 + h], ypair)
    cross_kept(ga, gb, 3, OWN3, T3, P3, yl)
    last_step()
    for h in range(2):
        cross_in(gb, h, 4, ry.at[2 + h])
        cross_out(gb, h, OTHER2, 6, sx, rx.at[2 + h], xpair)
    cross_kept(gb, gc, 2, OWN2, T2, P2, x % 2)
    arrived(R.at[pl.ds(0, 3), :, 0], rS.at[1])
    px_send(True, 0)
    px_send(True, 1, False)
    for h in range(2):
        cross_in(gc, h, 6, rx.at[2 + h])
    reduce_middle(3)
    local_back(gc, gb, 1, T1)
    local_back(gb, ga, 0, T0)
    grad_tokens_out = local(ga, grad_tokens_hbm, 5)
    grad_tokens_out.start()
    reduce_middle(2)
    reduce_middle(1)
    reduce_middle(0)
    px_last(0)
    px_send(True, 1, True)
    pl.when(own_s >= 2)(own_work)
    pl.when(own_s < 2)(own_work)
    px_last(1)
    px_own(True)
    for s in (3, 2, 1, 0):
        @pl.when(own_s != s)
        def _():
            arrived(ain.at[pl.ds(0, 4)], rF.at[s])

        @pl.when(own_s == s)
        def _():
            arrived(ain.at[pl.ds(0, 3)], rF.at[s])

        send(fout.at[core, s], fout.at[core, s], sH, rH.at[s], sibling)
        grad_factors[s, pl.ds(32 * core, 32), :] = fout[core, s].astype(F32)
    factors_out = [local(grad_factors.at[s], grad_factors_hbm.at[s], 7 + s) for s in range(4)]
    for s in (3, 2, 1, 0):
        arrived(fout.at[1 - core, s], rH.at[s])
        grad_factors[s, pl.ds(32 - 32 * core, 32), :] = fout[1 - core, s].astype(F32)
        factors_out[s].start()

    for i, nu, nd in ((0, 1, 2), (1, 2, 1)):
        for h in range(2):
            px_arrived(0, nu, h)
            px_arrived(1, nd, h)
        total = pbuf[i] + px_in[0, nu].astype(F32) + px_in[1, nd].astype(F32)
        proj[pl.ds(256 * i, 256), :] = total.astype(BF16)

    proj_out = local(proj, proj_hbm, 6)
    proj_out.start()
    for copy in (grad_tokens_out, proj_out, *factors_out):
        copy.wait()
    all_sent(zsend.at[pl.ds(0, 2)], sx)
    all_sent(zsend.at[pl.ds(0, 2)], sy)
    all_sent(px_out, sc)
    all_sent(w_oth, sw)
    for b in range(2):
        pl.when(jnp.logical_not((yh == b) & diagonal))(lambda: all_sent(rot, sys.at[b]))
        all_sent(up_out, sR.at[b])
        all_sent(up_out, sZ.at[b])
    all_sent(bsib, sS)
    all_sent(bsib, sB)
    all_sent(px_out, sP)
    pl.when(off_diagonal)(lambda: all_sent(rot, sG.at[0]))
    all_sent(rot, sG.at[1])
    all_sent(cin, sC)
    all_sent(ain.at[pl.ds(0, 15)], sA)
    all_sent(ain.at[pl.ds(0, 15)], sF)
    all_sent(fout.at[0], sH)


def hand_over(proj, grad_tokens, grad_factors, proj_out, tokens_out, factors_out, a, b, c, came, gone):
    parts = [(proj, a, proj_out, pl.ds(128 * i, 128)) for i in range(4)]
    parts += [(grad_factors, c, factors_out, i) for i in range(4)]
    parts.append((grad_tokens, b, tokens_out, pl.ds(0, 128)))
    into = [pltpu.make_async_copy(s.at[i], v.at[i], came.at[n]) for n, (s, v, d, i) in enumerate(parts)]
    out = [pltpu.make_async_copy(v.at[i], d.at[i], gone.at[n]) for n, (s, v, d, i) in enumerate(parts)]
    for copy in into:
        copy.start()
    for first, second in zip(into, out):
        first.wait()
        second.start()
    for copy in out:
        copy.wait()


def per_device(tokens, weight, factors, cotangent):
    V = pltpu.VMEM
    D = pltpu.SemaphoreType.DMA
    shapes = (
        jax.ShapeDtypeStruct((512, 896), BF16),
        jax.ShapeDtypeStruct((128, 768), F32),
        jax.ShapeDtypeStruct((4, 64, 768), F32),
    )
    hbm = pl.BlockSpec(memory_space=pl.ANY)
    results = pl.pallas_call(
        main_kernel,
        out_shape=shapes,
        in_specs=[hbm] * 4,
        out_specs=(hbm,) * 3,
        scratch_shapes=[
            V((128, 768), BF16),
            V((4, 64, 768), F32),
            V((512, 896), BF16),
            V((4, 64, 768), F32),
            V((768, 896), BF16),
            V((2, 6, 3, 256, 256), BF16),
            V((9, 768, 128), BF16),
            *[V((128, 768), F32)] * 6,
            V((4, 64, 768), F32),
            V((4, 32, 768), F32),
            V((4, 32, 768), F32),
            V((4, 32, 768), BF16),
            V((16, 16, 384), BF16),
            V((16, 384), BF16),
            V((2, 4, 32, 768), BF16),
            V((8, 128, 768), BF16),
            V((128, 768), BF16),
            V((8, 2, 2, 128, 768), BF16),
            V((8, 256, 896), BF16),
            V((768, 896), BF16),
            V((8, 2, 128, 768), BF16),
            V((8, 2, 128, 768), BF16),
            V((8, 2, 128, 768), F32),
            *[V((14, 64, 768), BF16)] * 4,
            V((2, 256, 896), F32),
            V((2, 128, 896), F32),
            V((2, 3, 256, 896), BF16),
            V((2, 3, 256, 896), BF16),
            V((2, 128, 768), BF16),
            V((2, 128, 768), BF16),
            D((11,)),
            D, D((4,)), D, D((4,)),
            D, D((6,)), D, D,
            D((2,)), D((2, 2)),
            D((2,)), D((2, 4, 2)),
            D, D((2,)),
            D, D((8, 2)),
            D((2,)), D((2, 14)),
            D, D((2, 6)),
            D((2,)), D((2, 2)),
            D, D((4,)),
            D, D,
            D, D((4,)),
            D, D((4,)),
        ],
        compiler_params=pltpu.CompilerParams(
            collective_id=0, has_side_effects=True, vmem_limit_bytes=60 * 1024 * 1024
        ),
        name="rotate_project",
    )(tokens, factors, weight, cotangent)
    return pl.pallas_call(
        hand_over,
        out_shape=shapes,
        in_specs=[hbm] * 3,
        out_specs=(hbm,) * 3,
        scratch_shapes=[
            V((512, 896), BF16),
            V((128, 768), F32),
            V((4, 64, 768), F32),
            D((9,)),
            D((9,)),
        ],
        compiler_params=pltpu.CompilerParams(vmem_limit_bytes=62 * 1024 * 1024),
        name="hand_over",
    )(*results)


def solution(mesh):
    placed = (P("dp", "tensor"), P("tensor", "dp"), P(None, None, "tensor"), P("tensor", "dp"))
    return jax.shard_map(
        per_device,
        mesh=mesh,
        in_specs=placed,
        out_specs=(P("tensor", "dp"), P("dp", "tensor"), P(None, None, "tensor")),
        check_vma=False,
    )
```

```python
import jax
import jax.numpy as jnp
from jax import lax
from jax.experimental import pallas as pl
from jax.experimental.pallas import tpu as pltpu
from jax.sharding import PartitionSpec as P

F32 = jnp.float32
BF16 = jnp.bfloat16
MESH = pl.DeviceIdType.MESH
Q = [pl.ds(128 * q, 128) for q in range(6)]
U = [pl.ds(256 * u, 256) for u in range(3)]
H = [pl.ds(64 * h, 64) for h in range(2)]
PX = [pl.ds(128 * h, 128) for h in range(2)]
M0, M1, OWN2, OTHER2, OWN3, OTHER3 = range(6)
T0, T1, T2, T3, P2, P3 = 0, 1, 3, 5, 7, 8


def dot(a, b, dims=((1,), (0,))):
    return lax.dot_general(a, b, (dims, ((), ())), preferred_element_type=F32)


def split(a):
    high = a.astype(BF16)
    return high, (a - high.astype(F32)).astype(BF16)


def block_masks():
    r = lax.broadcasted_iota(jnp.int32, (128, 128), 0) // 32
    c = lax.broadcasted_iota(jnp.int32, (128, 128), 1) // 32
    return (r // 2 == c // 2, r % 2 == c % 2, r == c)


def fold_cross(full, masks):
    full = jnp.where(masks[2], full, 0.0)
    return full[:32] + full[32:64] + full[64:96] + full[96:]


def main_kernel(
    tokens_hbm, factors_hbm, w_hbm, cot_hbm,
    proj_hbm, grad_tokens_hbm, grad_factors_hbm,
    tokens, factors, proj, grad_factors, w_own, mats, flipped, z1, z2, z3, ga, gb, gc, gf, cin, gh, ghb, ain, res, fout,
    zsend, rot, R, cotG, w_oth, bsib, bsib_in, bown, up_out, up_in, dn_out, dn_in,
    pbuf, px_kept, px_out, px_in, gsend, gin,
    loc_sem, sx, rx, sy, ry, sc, rc, sw, rw, sys, yr, sR, rR, sS, rS, sB, rB, sZ, rZ, sP, rP,
    sG, rG, sC, rC, sA, rA, sF, rF, sH, rH,
):
    dp, tn = lax.axis_index("dp"), lax.axis_index("tensor")
    core, z, yh = dp % 2, dp // 2 % 8, dp // 16
    x, yl = tn % 4, tn // 4
    chip = yh * 8 + z

    def dev(yh=yh, z=z, core=core, yl=yl, x=x):
        return (yh * 16 + z * 2 + core, yl * 4 + x)

    def chip_dev(index):
        return dev(yh=index // 8, z=index % 8)

    xl, xr, xo = (x + 3) % 4, (x + 1) % 4, (x + 2) % 4
    right, left = dev(x=xr), dev(x=xl)
    xpair = dev(x=x + 1 - 2 * (x % 2))
    ypair = dev(yl=1 - yl)
    sibling = dev(core=1 - core)
    above, below = dev(z=(z + 1) % 8), dev(z=(z + 7) % 8)
    diagonal = yh == yl
    off_diagonal = jnp.logical_not(diagonal)

    def rcopy(src, dst, ssem, rsem, to):
        return pltpu.make_async_remote_copy(
            src_ref=src, dst_ref=dst, send_sem=ssem, recv_sem=rsem,
            device_id=to, device_id_type=MESH,
        )

    def send(src, dst, ssem, rsem, to):
        rcopy(src, dst, ssem, rsem, to).start()

    def arrived(dst, rsem):
        rcopy(dst, dst, rsem, rsem, sibling).wait_recv()

    def all_sent(same_bytes, ssem):
        rcopy(same_bytes, same_bytes, ssem, ssem, sibling).wait_send()

    def local(src, dst, n):
        return pltpu.make_async_copy(src, dst, loc_sem.at[n])

    first = [local(tokens_hbm, tokens, 0), local(factors_hbm, factors, 1)]
    for copy in first:
        copy.start()

    barrier = pltpu.get_barrier_semaphore()

    def greet(r, carry):
        pl.semaphore_signal(barrier, inc=1, device_id=chip_dev((chip + r) % 16), device_id_type=MESH)
        return carry

    lax.fori_loop(1, 16, greet, 0)
    for peer in (right, left, ypair, sibling):
        pl.semaphore_signal(barrier, inc=1, device_id=peer, device_id_type=MESH)
    for peer, here in (
        (dev(yh=0, yl=yh), (yh == 0) & diagonal),
        (dev(yh=1, yl=yh), (yh == 1) & diagonal),
        (dev(yh=yl, yl=0), (yl == 0) & diagonal),
        (dev(yh=yl, yl=1), (yl == 1) & diagonal),
    ):
        @pl.when(jnp.logical_not(here))
        def _():
            pl.semaphore_signal(barrier, inc=1, device_id=peer, device_id_type=MESH)

    own_cot = [local(cot_hbm.at[pl.ds(256 * i, 256)], cotG.at[2 * x + i], 2 + i) for i in range(2)]
    own_w = local(w_hbm, w_own, 4)
    own_w.start()
    for copy in own_cot:
        copy.start()
    for copy in first:
        copy.wait()

    masks = block_masks()
    nothing = jnp.zeros((128, 128), BF16)

    def put_matrix(place, q, stacked, mask):
        u, k = q // 2, q % 2
        rows, rest = pl.ds(128 * k, 128), pl.ds(128 * (1 - k), 128)
        for part, value in enumerate(split(jnp.where(mask, stacked, 0.0))):
            mats[part, place, u, rows, rows] = value
            mats[part, place, u, rows, rest] = nothing

    def put_cross(section, bit, own):
        for q, cols in enumerate(Q):
            for part, place in ((bit, own), (1 - bit, own + 1)):
                coeffs = factors[section, pl.ds(32 * part, 32), cols]
                put_matrix(place, q, jnp.concatenate([coeffs] * 4, 0), masks[2])

    def times(parts, place, u, dims=((1,), (0,))):
        high, low = mats[0, place, u], mats[1, place, u]
        total = dot(parts[0], high, dims) + dot(parts[0], low, dims)
        return total + dot(parts[1], high, dims) if len(parts) > 1 else total

    def times_back(parts, place, u):
        return times(parts, place, u, ((1,), (1,)))

    for q, cols in enumerate(Q):
        c0, c1 = factors[0, :, cols], factors[1, :, cols]
        put_matrix(M0, q, jnp.concatenate([c0, c0], 0), masks[0])
        put_matrix(M1, q, jnp.concatenate([c1[:32], c1[:32], c1[32:], c1[32:]], 0), masks[1])
    for u, cols in enumerate(U):
        field = tokens[:, cols]
        field = field.astype(F32) + times([field], M0, u)
        z1[:, cols] = field
        field = field + times(split(field), M1, u)
        z2[:, cols] = field
        zsend[0, :, cols] = field.astype(BF16)

    pl.semaphore_wait(barrier, 23 - 2 * diagonal.astype(jnp.int32))

    def send_w(i):
        rows = pl.ds(128 * i, 128)
        send(w_hbm.at[rows], w_oth.at[rows], sw, rw, ypair)

    for h in range(2):
        send(zsend.at[0, H[h]], zsend.at[2, H[h]], sx, rx.at[h], xpair)
    for i, to in ((0, right), (1, left), (1, right), (0, left)):
        n = i + (0 if to is right else 2)
        send(cot_hbm.at[pl.ds(256 * i, 256)], cotG.at[2 * x + i], sc, rc.at[n], to)
    send_w(0)
    put_cross(2, x % 2, OWN2)
    put_cross(3, yl, OWN3)
    for u, cols in enumerate(U):
        field = z2[:, cols]
        z3[:, cols] = field + times(split(field), OWN2, u)
    for h in range(2):
        arrived(zsend.at[2, H[h]], rx.at[h])
        for u, cols in enumerate(U):
            field = z3[H[h], cols] + times([zsend[2, H[h], cols]], OTHER2, u)
            z3[H[h], cols] = field
            zsend[1, H[h], cols] = field.astype(BF16)
        send(zsend.at[1, H[h]], zsend.at[3, H[h]], sy, ry.at[h], ypair)

    slot = (yl + yh) % 2

    def to_holder(b, h):
        src = rot.at[H[h]]
        dst = R.at[z, slot, core, H[h]]
        return rcopy(src, dst, sys.at[b], yr.at[slot, h], dev(yh=b, yl=yh))

    for u, cols in enumerate(U):
        field = z3[:, cols]
        gc[:, cols] = field + times(split(field), OWN3, u)
    for h in range(2):
        arrived(zsend.at[3, H[h]], ry.at[h])
        for u, cols in enumerate(U):
            rot[H[h], cols] = (gc[H[h], cols] + times([zsend[3, H[h], cols]], OTHER3, u)).astype(BF16)
        for b in range(2):
            pl.when(jnp.logical_not((yh == b) & diagonal))(to_holder(b, h).start)

    @pl.when(diagonal)
    def _():
        R[z, 0, core] = rot[...]

    def spread(zz, s, up, down, k):
        block = R.at[zz, s, core]
        if up:
            send(block, block, sR.at[0], rR.at[0, k, s], above)
        if down:
            send(block, block, sR.at[1], rR.at[1, k, s], below)
        send(block, block, sS, rS.at[int(k > 2)], sibling)

    @pl.when(off_diagonal)
    def _():
        for h in range(2):
            arrived(R.at[z, 0, core, H[h]], yr.at[0, h])
    spread(z, 0, True, True, 0)
    for h in range(2):
        arrived(R.at[z, 1, core, H[h]], yr.at[1, h])
    spread(z, 1, True, True, 0)
    for i in range(1, 6):
        send_w(i)

    arrived(cotG.at[2 * xl], rc.at[0])
    send(cotG.at[2 * xl], cotG.at[2 * xl], sc, rc.at[4], right)
    arrived(cotG.at[2 * xr + 1], rc.at[3])
    send(cotG.at[2 * xr + 1], cotG.at[2 * xr + 1], sc, rc.at[5], left)

    def step(k, onward):
        lo, hi = (z + 8 - k) % 8, (z + k) % 8
        for s in range(2):
            arrived(R.at[lo, s, core], rR.at[0, k - 1, s])
            spread(lo, s, onward or s == 0, False, k)
            arrived(R.at[hi, s, core], rR.at[1, k - 1, s])
            spread(hi, s, False, onward or s == 0, k)

    def sib_copy(zz, s):
        return rcopy(bsib.at[zz, s], bsib_in.at[zz, s], sB, rB.at[zz, s], sibling)

    def back_unit(xb, s):
        rows = cotG[pl.ds(2 * xb, 2)].reshape(512, 896)
        w = w_oth if s else w_own
        part = lax.dot_general(rows, w[...], (((1,), (1,)), ((), ())), preferred_element_type=F32)
        for c in range(2):
            @pl.when(core == c)
            def _():
                for i in range(2):
                    first, second = 256 * i + 128 * c, 256 * i + 128 * (1 - c)
                    bown[2 * xb + i, s] = part[first:first + 128]
                    bsib[2 * xb + i, s] = part[second:second + 128].astype(BF16)
        for i in range(2):
            sib_copy(2 * xb + i, s).start()

    for copy in own_cot:
        copy.wait()
    own_w.wait()
    back_unit(x, 0)
    for saved, place in ((z1, T1), (z2, T2), (z3, T3)):
        for cols in Q:
            high, low = split(saved[:, cols].T)
            flipped[place, cols] = high
            flipped[place + 1, cols] = low
    step(1, True)
    for cols in Q:
        flipped[T0, cols] = tokens[:, cols].astype(F32).T.astype(BF16)
        flipped[P2, cols] = zsend[2, :, cols].astype(F32).T.astype(BF16)
        flipped[P3, cols] = zsend[3, :, cols].astype(F32).T.astype(BF16)
    arrived(cotG.at[2 * xl + 1], rc.at[1])
    back_unit(xl, 0)
    arrived(cotG.at[2 * xr], rc.at[2])
    back_unit(xr, 0)
    step(2, False)
    arrived(cotG.at[2 * xo], rc.at[4])
    arrived(cotG.at[2 * xo + 1], rc.at[5])
    back_unit(xo, 0)

    def z_at(k):
        return (z + 8 + k) % 8

    def back_ready(s, *places):
        for k in places:
            arrived(bsib_in.at[z_at(k), s], rB.at[z_at(k), s])

    def own_back(zz, s, rows):
        return bown[zz, s, rows] + bsib_in[zz, s, rows].astype(F32)

    def ring_send(s, n):
        for direction in range(2):
            out, into = (dn_out, dn_in) if direction else (up_out, up_in)
            distance = 4 - (n + 1) // 2
            h = direction if n % 2 == 0 else 1 - direction
            value = own_back(z_at(-distance if direction else distance), s, H[h])
            if n >= 2:
                arrived(into.at[7 * s + n - 2], rZ.at[direction, 7 * s + n - 2])
                value = value + into[7 * s + n - 2].astype(F32)
            m = 7 * s + n
            out[m] = value.astype(BF16)
            send(out.at[m], into.at[m], sZ.at[direction], rZ.at[direction, m], below if direction else above)

    def to_owner(s, h):
        return rcopy(gsend.at[s, H[h]], gin.at[yh, H[h]], sG.at[s], rG.at[yh, h], dev(yh=yl, yl=(yl + s) % 2))

    def ring_end(s):
        for h in (1, 0):
            nu, nd = 7 * s + 6 - h, 7 * s + 5 + h
            arrived(up_in.at[nu], rZ.at[0, nu])
            arrived(dn_in.at[nd], rZ.at[1, nd])
            total = own_back(z, s, H[h]) + up_in[nu].astype(F32) + dn_in[nd].astype(F32)
            gsend[s, H[h]] = total.astype(BF16)
            if s == 1:
                to_owner(s, h).start()
            else:
                pl.when(off_diagonal)(to_owner(s, h).start)

                @pl.when(diagonal)
                def _():
                    gin[yh, H[h]] = gsend[0, H[h]]

    def product(zz):
        return jnp.dot(R[zz, 0].reshape(256, 768), w_own[...], preferred_element_type=F32) + jnp.dot(
            R[zz, 1].reshape(256, 768), w_oth[...], preferred_element_type=F32
        )

    def in_phase(zz, late):
        away = (zz - z + 8) % 8
        return ((away >= 3) & (away <= 5)) == late

    def px_place(direction, n):
        return ((2 * xo + 1, 2 * xr, 2 * xr + 1), (2 * xo, 2 * xl + 1, 2 * xl))[direction][n]

    def px_arrived(direction, n, h):
        arrived(px_in.at[direction, n, PX[h]], rP.at[direction, 2 * n + h])

    def px_post(direction, n, h, part):
        if n == 2:
            px_arrived(direction, 0, h)
            part = part + px_in[direction, 0, PX[h]].astype(F32)
        px_out[direction, n, PX[h]] = part.astype(BF16)
        send(
            px_out.at[direction, n, PX[h]], px_in.at[direction, n, PX[h]], sP,
            rP.at[direction, 2 * n + h], left if direction else right,
        )

    def px_send(late, n, after_far=None):
        for direction in range(2):
            now = in_phase(px_place(direction, n), late)
            if after_far is not None:
                now = now & in_phase(px_place(direction, 0), after_far)

            @pl.when(now)
            def _():
                value = product(px_place(direction, n))
                for h in range(2):
                    px_post(direction, n, h, value[128 * h:128 * h + 128])

    def px_last(h):
        for direction in range(2):
            @pl.when(in_phase(px_place(direction, 2), True))
            def _():
                if h == 0:
                    value = product(px_place(direction, 2))
                    px_post(direction, 2, 0, value[:128])
                    px_kept[direction] = value[128:]
                else:
                    px_post(direction, 2, 1, px_kept[direction])

    def px_own(late):
        for i in range(2):
            @pl.when(in_phase(2 * x + i, late))
            def _():
                pbuf[i] = product(2 * x + i)

    def third_step(s):
        lo, hi = z_at(-3), z_at(3)
        arrived(R.at[lo, s, core], rR.at[0, 2, s])
        spread(lo, s, False, False, 3)
        arrived(R.at[hi, s, core], rR.at[1, 2, s])
        spread(hi, s, False, s == 1, 3)

    def last_step():
        zf = z_at(4)
        for s in range(2):
            arrived(R.at[zf, s, core], rR.at[s, 3, s])
            spread(zf, s, False, False, 4)

    back_ready(0, 4, 3, -3)
    ring_send(0, 0)
    ring_send(0, 1)
    back_ready(0, 2, -2, 1, -1, 0)
    ring_send(0, 2)
    ring_send(0, 3)
    arrived(w_oth, rw)
    far = z_at(4) // 2
    turn = 2 * (z % 2) - 1
    back_unit(far, 1)
    ring_send(0, 4)
    arrived(R.at[pl.ds(0, 5), :, 0], rS.at[0])
    px_send(False, 0)
    ring_send(0, 5)
    back_unit((far + 4 + turn) % 4, 1)
    ring_send(0, 6)
    back_ready(1, 4, 3, -3)
    ring_send(1, 0)
    ring_send(1, 1)
    back_unit((far + 4 - turn) % 4, 1)
    third_step(0)
    back_unit((far + 2) % 4, 1)
    px_send(False, 1)
    ring_send(1, 2)
    ring_end(0)
    back_ready(1, 2, -2)
    ring_send(1, 3)
    px_send(False, 2)
    ring_send(1, 4)
    back_ready(1, 1, -1, 0)
    ring_send(1, 5)
    px_own(False)
    ring_send(1, 6)
    ring_end(1)
    held = ((z_at(-2), 1, 0, 2, above), (z_at(2), 1, 1, 2, below), (z_at(-3), 0, 0, 3, above))
    for zz, s, direction, k, to in held:
        block = R.at[zz, s, core]
        send(block, block, sR.at[direction], rR.at[direction, k, s], to)
    pl.when(off_diagonal)(lambda: third_step(1))

    def reduce_start(s):
        send(gf.at[s, pl.ds(32 * (1 - core), 32)], cin.at[s], sC, rC.at[s], sibling)

    def piece(j):
        return (pl.ds(16 * (j // 2), 16), pl.ds(384 * (j % 2), 384))

    def owner_of(s, j):
        return 8 * (j % 2) + 4 * (j // 2) + s

    def owner_copy(s, j):
        owner = owner_of(s, j)
        r = (chip + 16 - owner) % 16
        src = ghb.at[s, piece(j)[0], piece(j)[1]]
        return r, rcopy(src, ain.at[(r + 15) % 16], sA, rA, chip_dev(owner))

    def reduce_middle(s):
        arrived(cin.at[s], rC.at[s])
        gh[s] = gf[s, pl.ds(32 * core, 32), :] + cin[s]
        ghb[s] = gh[s].astype(BF16)
        for j in range(4):
            r, copy = owner_copy(s, j)
            pl.when(r != 0)(copy.start)

    own_s = z % 4
    own_rows, own_cols = pl.ds(16 * (z // 4), 16), pl.ds(384 * yh, 384)

    def peer_copy(r):
        place = fout.at[core, own_s, own_rows, own_cols]
        return rcopy(res, place, sF, rF.at[own_s], chip_dev((chip + r) % 16))

    def own_work():
        arrived(ain.at[pl.ds(0, 15)], rA)

        def add(r, total):
            return total + ain[r - 1].astype(F32)

        total = lax.fori_loop(1, 16, add, gh[own_s, own_rows, own_cols])
        res[...] = total.astype(BF16)
        fout[core, own_s, own_rows, own_cols] = res[...]

        for r in (4, 12, 3, 5, 11, 13, 2, 6, 10, 14, 1, 7, 9, 15, 8):
            peer_copy(r).start()

    def cross_out(g, h, other, a, ssem, rsem, peer):
        for u, cols in enumerate(U):
            zsend[a, H[h], cols] = times_back(split(g[H[h], cols]), other, u).astype(BF16)
        send(zsend.at[a, H[h]], zsend.at[a + 1, H[h]], ssem, rsem, peer)

    def products_with(parts, place, u, exact):
        total = dot(flipped[place, U[u]], parts[0]) + dot(flipped[place, U[u]], parts[1])
        return total if exact else total + dot(flipped[place + 1, U[u]], parts[0])

    def diagonals(full, u):
        return ((full[:128, :128], Q[2 * u]), (full[128:, 128:], Q[2 * u + 1]))

    def cross_kept(g, out, section, own, saved, partner, bit):
        for u, cols in enumerate(U):
            field = g[:, cols]
            parts = split(field)
            out[:, cols] = field + times_back(parts, own, u)
            for place, exact, side in ((saved, False, bit), (partner, True, 1 - bit)):
                for full, q in diagonals(products_with(parts, place, u, exact), u):
                    gf[section, pl.ds(32 * side, 32), q] = fold_cross(full, masks)
        reduce_start(section)

    def cross_in(out, h, a, rsem):
        arrived(zsend.at[a + 1, H[h]], rsem)
        out[H[h]] += zsend[a + 1, H[h]].astype(F32)

    def local_back(g, out, section, saved):
        for u, cols in enumerate(U):
            field = g[:, cols]
            parts = split(field)
            out[:, cols] = field + times_back(parts, section, u)
            for full, q in diagonals(products_with(parts, saved, u, section == 0), u):
                full = jnp.where(masks[section], full, 0.0)
                if section == 0:
                    gf[0, :, q] = full[:64] + full[64:]
                else:
                    gf[1, pl.ds(0, 32), q] = full[:32] + full[32:64]
                    gf[1, pl.ds(32, 32), q] = full[64:96] + full[96:]
        reduce_start(section)

    for h in range(2):
        for a in range(2):
            @pl.when(jnp.logical_not((yh == a) & diagonal))
            def _():
                arrived(gin.at[a, H[h]], rG.at[a, h])
        ga[H[h]] = gin[0, H[h]].astype(F32) + gin[1, H[h]].astype(F32)
        cross_out(ga, h, OTHER3, 4, sy, ry.at[2 + h], ypair)
    cross_kept(ga, gb, 3, OWN3, T3, P3, yl)
    pl.when(diagonal)(lambda: third_step(1))
    last_step()
    for h in range(2):
        cross_in(gb, h, 4, ry.at[2 + h])
        cross_out(gb, h, OTHER2, 6, sx, rx.at[2 + h], xpair)
    cross_kept(gb, gc, 2, OWN2, T2, P2, x % 2)
    arrived(R.at[pl.ds(0, 3), :, 0], rS.at[1])
    px_send(True, 0)
    px_send(True, 1, False)
    for h in range(2):
        cross_in(gc, h, 6, rx.at[2 + h])
    reduce_middle(3)
    local_back(gc, gb, 1, T1)
    local_back(gb, ga, 0, T0)
    grad_tokens_out = local(ga, grad_tokens_hbm, 5)
    grad_tokens_out.start()
    reduce_middle(2)
    reduce_middle(1)
    reduce_middle(0)
    px_last(0)
    px_send(True, 1, True)
    pl.when(own_s >= 2)(own_work)
    px_last(1)
    pl.when(own_s < 2)(own_work)
    px_own(True)
    for s in (3, 2, 1, 0):
        @pl.when(own_s != s)
        def _():
            arrived(ain.at[pl.ds(0, 4)], rF.at[s])

        @pl.when(own_s == s)
        def _():
            arrived(ain.at[pl.ds(0, 3)], rF.at[s])

        send(fout.at[core, s], fout.at[core, s], sH, rH.at[s], sibling)
        grad_factors[s, pl.ds(32 * core, 32), :] = fout[core, s].astype(F32)
    factors_out = [local(grad_factors.at[s], grad_factors_hbm.at[s], 7 + s) for s in range(4)]
    for s in (3, 2, 1, 0):
        arrived(fout.at[1 - core, s], rH.at[s])
        grad_factors[s, pl.ds(32 - 32 * core, 32), :] = fout[1 - core, s].astype(F32)
        factors_out[s].start()

    for i, nu, nd in ((0, 1, 2), (1, 2, 1)):
        for h in range(2):
            px_arrived(0, nu, h)
            px_arrived(1, nd, h)
        total = pbuf[i] + px_in[0, nu].astype(F32) + px_in[1, nd].astype(F32)
        proj[pl.ds(256 * i, 256), :] = total.astype(BF16)

    proj_out = local(proj, proj_hbm, 6)
    proj_out.start()
    for copy in (grad_tokens_out, proj_out, *factors_out):
        copy.wait()
    all_sent(zsend.at[pl.ds(0, 2)], sx)
    all_sent(zsend.at[pl.ds(0, 2)], sy)
    all_sent(px_out, sc)
    all_sent(w_oth, sw)
    for b in range(2):
        pl.when(jnp.logical_not((yh == b) & diagonal))(lambda: all_sent(rot, sys.at[b]))
        all_sent(up_out, sR.at[b])
        all_sent(up_out, sZ.at[b])
    all_sent(bsib, sS)
    all_sent(bsib, sB)
    all_sent(px_out, sP)
    pl.when(off_diagonal)(lambda: all_sent(rot, sG.at[0]))
    all_sent(rot, sG.at[1])
    all_sent(cin, sC)
    all_sent(ain.at[pl.ds(0, 15)], sA)
    all_sent(ain.at[pl.ds(0, 15)], sF)
    all_sent(fout.at[0], sH)


def hand_over(proj, grad_tokens, grad_factors, proj_out, tokens_out, factors_out, a, b, c, came, gone):
    parts = [(proj, a, proj_out, pl.ds(128 * i, 128)) for i in range(4)]
    parts += [(grad_factors, c, factors_out, i) for i in range(4)]
    parts.append((grad_tokens, b, tokens_out, pl.ds(0, 128)))
    into = [pltpu.make_async_copy(s.at[i], v.at[i], came.at[n]) for n, (s, v, d, i) in enumerate(parts)]
    out = [pltpu.make_async_copy(v.at[i], d.at[i], gone.at[n]) for n, (s, v, d, i) in enumerate(parts)]
    for copy in into:
        copy.start()
    for first, second in zip(into, out):
        first.wait()
        second.start()
    for copy in out:
        copy.wait()


def per_device(tokens, weight, factors, cotangent):
    V = pltpu.VMEM
    D = pltpu.SemaphoreType.DMA
    shapes = (
        jax.ShapeDtypeStruct((512, 896), BF16),
        jax.ShapeDtypeStruct((128, 768), F32),
        jax.ShapeDtypeStruct((4, 64, 768), F32),
    )
    hbm = pl.BlockSpec(memory_space=pl.ANY)
    results = pl.pallas_call(
        main_kernel,
        out_shape=shapes,
        in_specs=[hbm] * 4,
        out_specs=(hbm,) * 3,
        scratch_shapes=[
            V((128, 768), BF16),
            V((4, 64, 768), F32),
            V((512, 896), BF16),
            V((4, 64, 768), F32),
            V((768, 896), BF16),
            V((2, 6, 3, 256, 256), BF16),
            V((9, 768, 128), BF16),
            *[V((128, 768), F32)] * 6,
            V((4, 64, 768), F32),
            V((4, 32, 768), F32),
            V((4, 32, 768), F32),
            V((4, 32, 768), BF16),
            V((16, 16, 384), BF16),
            V((16, 384), BF16),
            V((2, 4, 32, 768), BF16),
            V((8, 128, 768), BF16),
            V((128, 768), BF16),
            V((8, 2, 2, 128, 768), BF16),
            V((8, 256, 896), BF16),
            V((768, 896), BF16),
            V((8, 2, 128, 768), BF16),
            V((8, 2, 128, 768), BF16),
            V((8, 2, 128, 768), F32),
            *[V((14, 64, 768), BF16)] * 4,
            V((2, 256, 896), F32),
            V((2, 128, 896), F32),
            V((2, 3, 256, 896), BF16),
            V((2, 3, 256, 896), BF16),
            V((2, 128, 768), BF16),
            V((2, 128, 768), BF16),
            D((11,)),
            D, D((4,)), D, D((4,)),
            D, D((6,)), D, D,
            D((2,)), D((2, 2)),
            D((2,)), D((2, 4, 2)),
            D, D((2,)),
            D, D((8, 2)),
            D((2,)), D((2, 14)),
            D, D((2, 6)),
            D((2,)), D((2, 2)),
            D, D((4,)),
            D, D,
            D, D((4,)),
            D, D((4,)),
        ],
        compiler_params=pltpu.CompilerParams(
            collective_id=0, has_side_effects=True, vmem_limit_bytes=60 * 1024 * 1024
        ),
        name="rotate_project",
    )(tokens, factors, weight, cotangent)
    return pl.pallas_call(
        hand_over,
        out_shape=shapes,
        in_specs=[hbm] * 3,
        out_specs=(hbm,) * 3,
        scratch_shapes=[
            V((512, 896), BF16),
            V((128, 768), F32),
            V((4, 64, 768), F32),
            D((9,)),
            D((9,)),
        ],
        compiler_params=pltpu.CompilerParams(vmem_limit_bytes=62 * 1024 * 1024),
        name="hand_over",
    )(*results)


def solution(mesh):
    placed = (P("dp", "tensor"), P("tensor", "dp"), P(None, None, "tensor"), P("tensor", "dp"))
    return jax.shard_map(
        per_device,
        mesh=mesh,
        in_specs=placed,
        out_specs=(P("tensor", "dp"), P("dp", "tensor"), P(None, None, "tensor")),
        check_vma=False,
    )
```
